512 devices in a mesh: src: 8 (over x, y_lo), gx: 16 (over z, core), gy: 4 (over y_hi).
Axes of the slice: x: 4, y: 8 (y_hi: 4, y_lo: 2; y = y_hi * 2 + y_lo), z: 8, core: 2. Of those that a mesh axis runs over, the one named last changes fastest.
Arguments:
- warm_potential: float32 [32, 64, 128, 128], P('src', 'gx', 'gy'), may hold values from -3 to 3
- warm_adjoint: float32 [32, 64, 128, 128], P('src', 'gx', 'gy'), may hold values from -3 to 3
- conductivity: float32 [64, 128, 128], P('gx', 'gy', 'src'), may hold values from 0.2 to 5
- electrodes: int32 [32, 2], replicated, may hold values from 0 to 8191
- receivers: int32 [128, 2], replicated, may hold values from 0 to 8191
- observed: float32 [32, 128], replicated, may hold values from -6 to 6
- source_order: int32 [32], replicated, may hold values from 0 to 31, each once
Outputs:
- gradient: float32 [64, 128, 128], P('gx', 'gy', 'src')
The draws below stay inside these ranges and needn't reach their ends.
Inputs may be any that keep to these rules, and one draw needn't show every extreme that they name: `electrodes`: entries number surface cells as x * 128 + y. `receivers`: entries number surface cells as x * 128 + y.
All inputs are finite; a program needn't handle non-finite values.
Results may differ from the reference program's by a relative error of at most 0.0003.
Values sent between devices are 32-bit elements; how exact they have to be, the bound alone decides.
A program may use at most 64 MiB of HBM per device.

```python
import math
import jax
import jax.numpy as jnp
from jax import lax

NZ = 128
NREC = 128
SWEEPS = 6
NX = 64
NY = 128
NSRC = 32


def plant(drawn, key, low, top_value):
    place = [jax.random.randint(jax.random.fold_in(key, axis), (), 0, length) for axis, length in enumerate(drawn.shape)]
    widest = drawn.shape.index(max(drawn.shape))
    beside = place[:widest] + [(place[widest] + 1) % drawn.shape[widest]] + place[widest + 1:]
    return drawn.at[tuple(place)].set(low).at[tuple(beside)].set(top_value)


def block_levels(stream_key, shape, shards, least, top_value):
    factor_of = 1.0
    for axis_at, shards_of in shards:
        draws = jax.random.uniform(jax.random.fold_in(jax.random.fold_in(stream_key, 6), axis_at), (shards_of,), jnp.float32, least / len(shards), top_value / len(shards))
        factor_of = factor_of * jnp.repeat(jnp.exp(draws), shape[axis_at] // shards_of).reshape((-1,) + (1,) * (len(shape) - 1 - axis_at))
    return factor_of


def gaussian(stream_key, extent, scale, limit, shards=(), kind=jnp.bfloat16):
    array = jax.random.normal(stream_key, extent, jnp.float32) * scale
    if len(shards) > 0:
        array = block_levels(stream_key, extent, shards, -0.22, 0.18) * array
    return jnp.clip(array, min=-limit, max=limit).astype(kind)


def setup_inputs(seed: int = 0) -> dict:
    arg_keys = jax.random.split(jax.random.key(seed), 8)
    warm_potential = gaussian(arg_keys[0], (NSRC, NX, NY, NZ), 0.5, 3.0, ((0, 8), (1, 16), (2, 4)), jnp.float32)
    warm_adjoint = gaussian(arg_keys[1], (NSRC, NX, NY, NZ), 0.5, 3.0, ((0, 8), (1, 16), (2, 4)), jnp.float32)
    conductivity = jnp.clip(jnp.exp(math.log(5.0) - 3.218876 * jax.random.uniform(arg_keys[2], (NX, NY, NZ), jnp.float32) ** block_levels(arg_keys[2], (NX, NY, NZ), ((0, 16), (1, 4), (2, 8)), -0.2, 0.2)), 0.2, 5.0)
    electrodes = plant(jax.random.randint(arg_keys[3], (NSRC, 2), 0, NX * NY), jax.random.fold_in(arg_keys[3], 1), 0, (NX * NY) - 1).astype(jnp.int32)
    receivers = plant(jax.random.randint(arg_keys[4], (NREC, 2), 0, NX * NY), jax.random.fold_in(arg_keys[4], 1), 0, (NX * NY) - 1).astype(jnp.int32)
    observed = gaussian(arg_keys[5], (NSRC, NREC), 1.0, 6.0, (), jnp.float32)
    source_order = jax.random.permutation(arg_keys[6], NSRC).astype(jnp.int32)
    return dict(warm_potential=warm_potential, warm_adjoint=warm_adjoint, conductivity=conductivity, electrodes=electrodes, receivers=receivers, observed=observed, source_order=source_order)


lowest = 0.05
highest = 2.0
centre = (highest + lowest) / 2.0
half_span = (highest - lowest) / 2.0
bound_ratio = centre / half_span
strength = 4.0


def harmonic(left, right):
    return jnp.where(right > 0, 2.0 * left * right / (left + right), left)


def slope_of(left, right):
    total = left + right
    return jnp.where(right > 0, 2.0 * right * right / (total * total), 1.0)


def neighbours(field, padded):
    widths = [(0, 0)] * (field.ndim - 1) + [(1, 1)]
    deeper = jnp.pad(field, widths)
    return (padded[..., :-2, 1:-1, :], padded[..., 2:, 1:-1, :], padded[..., 1:-1, :-2, :],
            padded[..., 1:-1, 2:, :], deeper[..., :-2], deeper[..., 2:])


def face_tables(sigma, padded):
    others = neighbours(sigma, padded)
    depth = lax.broadcasted_iota(jnp.int32, sigma.shape, 2)
    surface = depth == 0
    coeffs = [harmonic(sigma, other) for other in others]
    slopes = [slope_of(sigma, other) for other in others]
    coeffs[4] = jnp.where(surface, 0.0, coeffs[4])
    slopes[4] = jnp.where(surface, 0.0, slopes[4])
    return coeffs, slopes


def apply_operator(field, padded, coeffs):
    others = neighbours(field, padded)
    total = coeffs[0] * (field - others[0])
    for index in range(1, 6):
        total = total + coeffs[index] * (field - others[index])
    return total


def solve(rhs, start, coeffs, inverse, pad_fn):
    residual = rhs - apply_operator(start, pad_fn(start), coeffs)
    update = inverse * residual / centre
    iterate = start
    factor = 1.0 / bound_ratio
    for sweep in range(SWEEPS):
        iterate = iterate + update
        residual = residual - apply_operator(update, pad_fn(update), coeffs)
        following = 1.0 / (2.0 * bound_ratio - factor)
        update = (following * factor) * update + (2.0 * following / half_span) * (inverse * residual)
        factor = following
    return iterate + update


def gradient_term(potential, adjoint, padded_potential, padded_adjoint, slopes):
    near_potential = neighbours(potential, padded_potential)
    near_adjoint = neighbours(adjoint, padded_adjoint)
    total = slopes[0] * (potential - near_potential[0]) * (adjoint - near_adjoint[0])
    for index in range(1, 6):
        total = total + slopes[index] * (potential - near_potential[index]) * (adjoint - near_adjoint[index])
    return total


def pad_plain(field):
    return jnp.pad(field, ((1, 1), (1, 1), (0, 0)))


def on_surface(flat):
    field = jnp.zeros((NX, NY, NZ), jnp.float32)
    return field.at[:, :, 0].set(flat.reshape(NX, NY))


def reference(warm_potential, warm_adjoint, conductivity, electrodes, receivers, observed, source_order):
    coeffs, slopes = face_tables(conductivity, pad_plain(conductivity))
    inverse = 1.0 / (coeffs[0] + coeffs[1] + coeffs[2] + coeffs[3] + coeffs[4] + coeffs[5])
    plus_cells = receivers[:, 0]
    minus_cells = receivers[:, 1]

    def one_source(total, slot):
        ident = source_order[slot]
        pair = electrodes[ident]
        surface = jnp.zeros((NX * NY,), jnp.float32).at[pair[0]].add(strength).at[pair[1]].add(-strength)
        potential = solve(on_surface(surface), warm_potential[slot], coeffs, inverse, pad_plain)
        top = potential[:, :, 0].reshape(-1)
        misfit = top[plus_cells] - top[minus_cells] - observed[ident]
        back = jnp.zeros((NX * NY,), jnp.float32).at[plus_cells].add(misfit).at[minus_cells].add(-misfit)
        adjoint = solve(on_surface(back), warm_adjoint[slot], coeffs, inverse, pad_plain)
        term = gradient_term(potential, adjoint, pad_plain(potential), pad_plain(adjoint), slopes)
        return total - term, None

    start = jnp.zeros((NX, NY, NZ), jnp.float32)
    gradient, unused = lax.scan(one_source, start, jnp.arange(NSRC, dtype=jnp.int32))
    return gradient
```

```python
import functools

import jax
import jax.numpy as jnp
from jax import lax
from jax.experimental import pallas as pl
from jax.experimental.pallas import tpu as pltpu
from jax.sharding import PartitionSpec as P

MESH = pl.DeviceIdType.MESH
SWEEPS = 6
lowest = 0.05
highest = 2.0
centre = (highest + lowest) / 2.0
half_span = (highest - lowest) / 2.0
bound_ratio = centre / half_span
strength = 4.0

F32 = jnp.float32
I32 = jnp.int32
BF16 = jnp.bfloat16

NSRCG, NGX, NGY = 8, 16, 4
NZC = NGX // 2
NX, NY = 64, 128
XR, YR = 4, 32
CX = 2 * XR
HALO = 8
EX, EY = CX + 2 * HALO, YR + 2 * HALO


def chebyshev():
    out = []
    factor = 1.0 / bound_ratio
    for _ in range(SWEEPS):
        following = 1.0 / (2.0 * bound_ratio - factor)
        out.append((following * factor, 2.0 * following / half_span))
        factor = following
    return out


STEPS = chebyshev()


def split3(v):
    hi = v.astype(BF16)
    rest = v - hi.astype(F32)
    mid = rest.astype(BF16)
    lo = (rest - mid.astype(F32)).astype(BF16)
    return hi, mid, lo


def kernel(
    wp_ref, wa_ref, cond_ref, elec_ref, rec_ref, obs_ref, order_ref,
    out_ref,
    p0, p1, a0, a1, cext, coef, slope, gath, pan, pick, pick_own,
    scond, scoef, sinv, srhs, y0, y1, vm, zbuf, gbuf, gt, rbuf,
    loc_sem, warm_s, warm_r, cond_s, cond_r, src_s, src_r, z_s, z_r, g_s, g_r, rs_s, rs_r,
):
    src = lax.axis_index("src")
    gx = lax.axis_index("gx")
    gy = lax.axis_index("gy")
    zc = gx // 2
    core = gx - 2 * zc

    def place(ds=0, dz=0, t=0, dg=0):
        z2 = lax.rem(zc + (dz % NZC), NZC)
        c2 = core if t == 0 else 1 - core
        return {
            "src": lax.rem(src + (ds % NSRCG), NSRCG),
            "gx": 2 * z2 + c2,
            "gy": lax.rem(gy + (dg % NGY), NGY),
        }

    halo = [
        (dz, t, dg)
        for dg in (0, 1, -1)
        for dz in (0, 1, -1)
        for t in (1, 0)
        if (dz, t, dg) != (0, 0, 0)
    ]

    partners = [place(dz=dz, t=t, dg=dg) for dz, t, dg in halo]
    partners += [place(ds=ds, t=t) for ds in range(1, NSRCG) for t in (0, 1)]
    partners += [place(dz=dz) for dz in range(2, NZC - 1)]
    partners += [place(dg=dg) for dg in range(2, NGY - 1)]
    barrier = pltpu.get_barrier_semaphore()
    for device in partners:
        pl.semaphore_signal(barrier, inc=1, device_id=device, device_id_type=MESH)

    own_x = pl.ds(HALO + XR * core, XR)
    half = pl.ds(2 * core, 2)
    own_p = pltpu.make_async_copy(wp_ref.at[half], p0.at[:, own_x, HALO : HALO + YR, :], loc_sem.at[0])
    own_a = pltpu.make_async_copy(wa_ref.at[half], a0.at[:, own_x, HALO : HALO + YR, :], loc_sem.at[1])
    own_p.start()
    own_a.start()

    own_rows = pl.ds(pl.multiple_of(16 * src, 16), 16)
    gath[own_rows, :] = cond_ref[...]

    pl.semaphore_wait(barrier, len(partners))

    gathers = [
        pltpu.make_async_remote_copy(
            cond_ref, gath.at[own_rows, :], src_s.at[ds - 1], src_r.at[ds - 1],
            device_id=place(ds=ds), device_id_type=MESH,
        )
        for ds in range(1, NSRCG)
    ]
    for copy in gathers:
        copy.start()

    def y_spans(dg):
        if dg == 0:
            return slice(0, YR), slice(HALO, HALO + YR)
        if dg == 1:
            return slice(YR - HALO, YR), slice(0, HALO)
        return slice(0, HALO), slice(HALO + YR, EY)

    def warm_copies(which, ref, dest):
        copies = []
        for dz, t, dg in halo:
            ys, yd = y_spans(dg)
            c2 = core if t == 0 else 1 - core
            copies.append(
                pltpu.make_async_remote_copy(
                    ref.at[pl.ds(2 * c2, 2), :, ys, :],
                    dest.at[:, pl.ds(HALO * (1 - dz) + XR * core, XR), yd, :],
                    warm_s.at[which, dz + 1, t, dg + 1],
                    warm_r.at[which, dz + 1, t, dg + 1],
                    device_id=place(dz=dz, t=t, dg=dg), device_id_type=MESH,
                )
            )
        return copies

    copies_p = warm_copies(0, wp_ref, p0)
    copies_a = warm_copies(1, wa_ref, a0)
    for copy in copies_p:
        copy.start()

    rx0 = rec_ref[:, 0:1] >> 7
    ry0 = rec_ref[:, 0:1] & (NY - 1)
    rx1 = rec_ref[:, 1:2] >> 7
    ry1 = rec_ref[:, 1:2] & (NY - 1)

    def own_flat(cx, cy):
        lx = cx - CX * zc
        ly = cy - YR * gy
        inside = (lx >= 0) & (lx < CX) & (ly >= 0) & (ly < YR)
        return jnp.where(inside, lx * YR + ly, -1)

    flats = lax.broadcasted_iota(I32, (128, CX * YR), 1)
    pick_own[...] = (
        jnp.where(own_flat(rx0, ry0) == flats, 1.0, 0.0)
        - jnp.where(own_flat(rx1, ry1) == flats, 1.0, 0.0)
    ).astype(BF16)

    lanes = lax.broadcasted_iota(I32, (128, 128), 1)
    ylane = lanes & 63
    ycell = (YR * gy - HALO + ylane) & (NY - 1)
    ok0 = (ry0 == ycell) & (ylane < EY)
    ok1 = (ry1 == ycell) & (ylane < EY)
    col0 = jnp.where(ok0, rx0, -1)
    col1 = jnp.where(ok1, rx1, -1)
    for r in range(EX):
        xrow = (CX * zc - HALO + r) & (NX - 1)
        pick[:, r * 128 : (r + 1) * 128] = (
            jnp.where(col0 == xrow, 1.0, 0.0) - jnp.where(col1 == xrow, 1.0, 0.0)
        ).astype(BF16)

    for copy in gathers:
        copy.wait_recv()
    pan[...] = jnp.transpose(gath[...]).reshape(XR, YR, 128)
    cext[own_x, HALO : HALO + YR, :] = pan[...]
    copies_c = []
    for dz, t, dg in halo:
        ys, yd = y_spans(dg)
        copies_c.append(
            pltpu.make_async_remote_copy(
                pan.at[:, ys, :],
                cext.at[pl.ds(HALO * (1 - dz) + XR * core, XR), yd, :],
                cond_s.at[dz + 1, t, dg + 1],
                cond_r.at[dz + 1, t, dg + 1],
                device_id=place(dz=dz, t=t, dg=dg), device_id_type=MESH,
            )
        )
    for copy in copies_c:
        copy.start()
    for copy in copies_a:
        copy.start()
    for copy in copies_c:
        copy.wait_recv()

    yy = (YR * gy - HALO + lax.broadcasted_iota(I32, (EY, 128), 0)) & (NY - 1)
    zz = lax.broadcasted_iota(I32, (EY, 128), 1)
    in_ym = yy != 0
    in_yp = yy != NY - 1
    in_zm = zz != 0
    in_zp = zz != 127

    def x_inside(r):
        row = (CX * zc - HALO + r) & (NX - 1)
        return jnp.where(row == 0, 0.0, 1.0).astype(F32), jnp.where(row == NX - 1, 0.0, 1.0).astype(F32)

    def harmonic(s, n):
        return 2.0 * s * n / (s + n)

    def coef_row(r, carry):
        s = cext[r]
        fm, fp = x_inside(r)
        hxm = harmonic(s, cext[r - 1]) * fm
        hxp = harmonic(s, cext[r + 1]) * fp
        hym = jnp.where(in_ym, harmonic(s, pltpu.roll(s, 1, 0)), 0.0)
        hyp = jnp.where(in_yp, harmonic(s, pltpu.roll(s, EY - 1, 0)), 0.0)
        hzm = jnp.where(in_zm, harmonic(s, pltpu.roll(s, 1, 1)), 0.0)
        hzp = jnp.where(in_zp, harmonic(s, pltpu.roll(s, 127, 1)), 0.0)
        diag = hxm + hxp + hym + hyp + hzm + hzp
        diag = diag + s * ((1.0 - fm) + (1.0 - fp))
        diag = diag + jnp.where(in_ym, 0.0, s) + jnp.where(in_yp, 0.0, s) + jnp.where(in_zp, 0.0, s)
        inv = 1.0 / diag
        for i, h in enumerate((hxm, hxp, hym, hyp, hzm, hzp)):
            coef[i, r] = h * inv
        return carry

    lax.fori_loop(1, EX - 1, coef_row, 0)

    def slope_of(s, n):
        total = s + n
        return 2.0 * n * n / (total * total)

    def slope_row(r, carry):
        s = cext[r]
        fm, fp = x_inside(r)
        q = r - HALO
        slope[0, q] = slope_of(s, cext[r - 1]) * fm + (1.0 - fm)
        slope[1, q] = slope_of(s, cext[r + 1]) * fp + (1.0 - fp)
        slope[2, q] = jnp.where(in_ym, slope_of(s, pltpu.roll(s, 1, 0)), 1.0)
        slope[3, q] = jnp.where(in_yp, slope_of(s, pltpu.roll(s, EY - 1, 0)), 1.0)
        slope[4, q] = jnp.where(in_zm, slope_of(s, pltpu.roll(s, 1, 1)), 0.0)
        slope[5, q] = jnp.where(in_zp, slope_of(s, pltpu.roll(s, 127, 1)), 1.0)
        return carry

    for first, count in ((0, 16), (16, 8)):
        gathered = jnp.ones((EY, 128), F32)
        for i in range(count):
            rolled = pltpu.roll(cext[first + i], 8 * i, 1) if i else cext[first]
            gathered = jnp.where((zz >= 8 * i) & (zz < 8 * i + 8), rolled, gathered)
        ones = jnp.ones((64 - EY, 128), F32)
        turned = jnp.transpose(jnp.concatenate([gathered, ones, gathered, ones], axis=0))
        scond[first : first + count] = turned[: 8 * count].reshape(count, 8, 128)

    shape = (EX - 2, 8, 128)
    lane3 = lax.broadcasted_iota(I32, shape, 2)
    sub3 = lax.broadcasted_iota(I32, shape, 1)
    row3 = (lax.broadcasted_iota(I32, shape, 0) + (CX * zc - HALO + 1)) & (NX - 1)
    y3 = (YR * gy - HALO + (lane3 & 63)) & (NY - 1)
    s = scond[1 : EX - 1]
    hs = [
        (harmonic(s, scond[0 : EX - 2]), row3 != 0, True),
        (harmonic(s, scond[2:EX]), row3 != NX - 1, True),
        (harmonic(s, pltpu.roll(s, 1, 2)), y3 != 0, True),
        (harmonic(s, pltpu.roll(s, 127, 2)), y3 != NY - 1, True),
        (harmonic(s, pltpu.roll(s, 1, 1)), sub3 != 0, False),
        (harmonic(s, pltpu.roll(s, 7, 1)), sub3 != 7, False),
    ]
    diag = jnp.zeros(shape, F32)
    for h, inside, outer in hs:
        diag = diag + jnp.where(inside, h, s if outer else 0.0)
    inv = 1.0 / diag
    sinv[...] = inv
    for i, (h, inside, outer) in enumerate(hs):
        scoef[i] = jnp.where(inside, h, 0.0) * inv

    def thin_solve():
        g = sinv[...] * srhs[...]
        zero = jnp.zeros((1, 8, 128), F32)
        for ref in (y0, y1):
            ref[0:1] = zero
            ref[EX - 1 : EX] = zero
        y0[1 : EX - 1] = jnp.zeros(shape, F32)
        y1[1 : EX - 1] = g * (1.0 / centre)
        older, newer = y0, y1
        for a, b in STEPS:
            u = newer[1 : EX - 1]
            total = scoef[0] * newer[0 : EX - 2] + scoef[1] * newer[2:EX]
            total = total + scoef[2] * pltpu.roll(u, 1, 2) + scoef[3] * pltpu.roll(u, 127, 2)
            total = total + scoef[4] * pltpu.roll(u, 1, 1) + scoef[5] * pltpu.roll(u, 7, 1)
            older[1 : EX - 1] = (1.0 + a - b) * u - a * older[1 : EX - 1] + b * (sinv[...] * srhs[...] + total)
            older, newer = newer, older
        return newer

    def add_thin(thin, dest):
        first = HALO - 1
        turned = jnp.transpose(thin[first : first + 16].reshape(128, 128))
        shallow = lanes < 8
        for i in range(CX + 2):
            part = jnp.where(shallow, pltpu.roll(turned, (128 - 8 * i) % 128, 1) if i else turned, 0.0)
            for slot in range(2):
                dest[slot, first + i] = dest[slot, first + i] + part[64 * slot : 64 * slot + EY]

    first_slot = 4 * src + 2 * core
    idents = [order_ref[first_slot + j] for j in range(2)]
    rhs = jnp.zeros(shape, F32)
    for e, sign in ((0, strength), (1, -strength)):
        cells = [elec_ref[k, e] for k in idents]
        ex = jnp.where(lane3 < 64, cells[0] >> 7, cells[1] >> 7)
        ey = jnp.where(lane3 < 64, cells[0] & (NY - 1), cells[1] & (NY - 1))
        hit = (ex == row3) & (ey == y3) & (sub3 == 0) & ((lane3 & 63) < EY)
        rhs = rhs + jnp.where(hit, sign, 0.0)
    srhs[...] = rhs
    thin_p = thin_solve()

    def full_solve(x0, x1):
        def app(x, prev, dest, wc, wu, wp, e):
            def row(r, carry):
                for slot in range(2):
                    u = x[slot, r]
                    total = coef[0, r] * x[slot, r - 1] + coef[1, r] * x[slot, r + 1]
                    total = total + coef[2, r] * pltpu.roll(u, 1, 0) + coef[3, r] * pltpu.roll(u, EY - 1, 0)
                    total = total + coef[4, r] * pltpu.roll(u, 1, 1) + coef[5, r] * pltpu.roll(u, 127, 1)
                    fresh = wu * u + wc * total
                    if prev is not None:
                        fresh = fresh - wp * prev[slot, r]
                    dest[slot, r] = fresh
                return carry

            lax.fori_loop(HALO - e, HALO + CX + e, row, 0)

        app(x0, None, x1, 1.0 / centre, 1.0 - 1.0 / centre, 0.0, HALO - 1)
        older, newer = x0, x1
        for k, (a, b) in enumerate(STEPS):
            app(newer, older, older, b, 1.0 + a - b, a, HALO - 2 - k)
            older, newer = newer, older
        return newer

    own_p.wait()
    for copy in copies_p:
        copy.wait_recv()
    pot = full_solve(p0, p1)
    add_thin(thin_p, pot)

    value = jnp.zeros((128, 128), F32)
    for slot in range(2):
        block = pot[slot, HALO : HALO + CX, HALO : HALO + YR, :].reshape(CX * YR, 128)
        got = jnp.zeros((128, 128), F32)
        for part in split3(block):
            got = got + jnp.dot(pick_own[...], part, preferred_element_type=F32)
        if slot:
            got = pltpu.roll(got, slot, 1)
        value = jnp.where(lanes == slot, got, value)
    vm[0] = jnp.transpose(value)[0:8]
    copies_z = [
        pltpu.make_async_remote_copy(
            vm.at[0], zbuf.at[dz - 1], z_s.at[dz - 1], z_r.at[dz - 1],
            device_id=place(dz=dz), device_id_type=MESH,
        )
        for dz in range(1, NZC)
    ]
    for copy in copies_z:
        copy.start()

    lax.fori_loop(HALO, HALO + CX, slope_row, 0)

    for copy in copies_z:
        copy.wait_recv()
    total = vm[0]
    for i in range(NZC - 1):
        total = total + zbuf[i]
    vm[1] = total
    copies_g = [
        pltpu.make_async_remote_copy(
            vm.at[1], gbuf.at[dg - 1], g_s.at[dg - 1], g_r.at[dg - 1],
            device_id=place(dg=dg), device_id_type=MESH,
        )
        for dg in range(1, NGY)
    ]
    for copy in copies_g:
        copy.start()

    own_a.wait()
    for copy in copies_a:
        copy.wait_recv()
    adj = full_solve(a0, a1)

    for copy in copies_g:
        copy.wait_recv()
    total = vm[1]
    for i in range(NGY - 1):
        total = total + gbuf[i]
    sub8 = lax.broadcasted_iota(I32, (8, 128), 0)
    lane8 = lax.broadcasted_iota(I32, (8, 128), 1)
    seen = jnp.where(sub8 == 0, obs_ref[pl.ds(idents[0], 1), :], obs_ref[pl.ds(idents[1], 1), :])
    misfit = jnp.where(sub8 < 2, total - seen, 0.0)
    hi, mid, lo = split3(misfit)
    stacked = jnp.concatenate(
        [hi.astype(F32), mid.astype(F32), lo.astype(F32), jnp.zeros((8, 128), F32)], axis=0
    ).astype(BF16)
    back = jnp.dot(stacked, pick[...], preferred_element_type=F32)
    for r in range(1, EX - 1):
        cut = back[:, r * 128 : (r + 1) * 128]
        both = cut[0:8] + cut[8:16] + cut[16:24]
        line = jnp.where(lane8[0:1] < 64, both[0:1], both[1:2])
        srhs[r - 1] = jnp.where(sub8 == 0, line, 0.0)
    add_thin(thin_solve(), adj)

    def grad_row(r, carry):
        q = r - HALO
        fm, fp = x_inside(r)
        sums = [jnp.zeros((EY, 128), F32) for _ in range(6)]
        for slot in range(2):
            p = pot[slot, r]
            a = adj[slot, r]
            near = [
                (pot[slot, r - 1] * fm, adj[slot, r - 1] * fm),
                (pot[slot, r + 1] * fp, adj[slot, r + 1] * fp),
            ]
            for inside, shift, axis in ((in_ym, 1, 0), (in_yp, EY - 1, 0), (in_zm, 1, 1), (in_zp, 127, 1)):
                near.append(
                    (
                        jnp.where(inside, pltpu.roll(p, shift, axis), 0.0),
                        jnp.where(inside, pltpu.roll(a, shift, axis), 0.0),
                    )
                )
            sums = [old + (p - pn) * (a - an) for old, (pn, an) in zip(sums, near)]
        out = slope[0, q] * sums[0]
        for i in range(1, 6):
            out = out + slope[i, q] * sums[i]
        pan8[q] = out[HALO : HALO + YR]
        return carry

    pan8 = slope.at[0, :, 0:YR, :]

    def grad_row_stored(r, carry):
        return grad_row(r, carry)

    lax.fori_loop(HALO, HALO + CX, grad_row_stored, 0)
    for c in range(2):
        gt[c] = jnp.transpose(slope[0, XR * c : XR * c + XR, 0:YR, :].reshape(128, 128))

    def rs_copy(ds, t):
        c2 = core if t == 0 else 1 - core
        s2 = lax.rem(src + ds, NSRCG)
        return pltpu.make_async_remote_copy(
            gt.at[c2, pl.ds(pl.multiple_of(16 * s2, 16), 16), :],
            rbuf.at[t, ds],
            rs_s.at[t, ds], rs_r.at[t, ds],
            device_id=place(ds=ds, t=t), device_id_type=MESH,
        )

    copies_rs = [rs_copy(ds, t) for ds in range(NSRCG) for t in (0, 1) if ds or t]
    for copy in copies_rs:
        copy.start()
    for copy in copies_rs:
        copy.wait_recv()
    total = gt[core, own_rows, :]
    for ds in range(NSRCG):
        for t in (0, 1):
            if ds or t:
                total = total + rbuf[t, ds]
    out_ref[...] = -total

    for copies in (gathers, copies_p, copies_a, copies_c, copies_z, copies_g, copies_rs):
        for copy in copies:
            copy.wait_send()


def body(warm_potential, warm_adjoint, conductivity, electrodes, receivers, observed, source_order):
    xr, yr, depth = conductivity.shape
    turned = conductivity.reshape(xr * yr, depth).T
    anyspace = pl.BlockSpec(memory_space=pl.ANY)
    vmem = pl.BlockSpec(memory_space=pltpu.VMEM)
    smem = pl.BlockSpec(memory_space=pltpu.SMEM)
    field = pltpu.VMEM((2, EX, EY, 128), F32)
    thin = pltpu.VMEM((EX, 8, 128), F32)
    inner = pltpu.VMEM((EX - 2, 8, 128), F32)
    dma = pltpu.SemaphoreType.DMA
    result = pl.pallas_call(
        kernel,
        out_shape=jax.ShapeDtypeStruct((16, 128), F32),
        in_specs=[anyspace, anyspace, vmem, smem, vmem, vmem, smem],
        out_specs=vmem,
        scratch_shapes=[
            field, field, field, field,
            pltpu.VMEM((EX, EY, 128), F32),
            pltpu.VMEM((6, EX, EY, 128), F32),
            pltpu.VMEM((6, CX, EY, 128), F32),
            pltpu.VMEM((128, 128), F32),
            pltpu.VMEM((XR, YR, 128), F32),
            pltpu.VMEM((128, EX * 128), BF16),
            pltpu.VMEM((128, CX * YR), BF16),
            thin,
            pltpu.VMEM((6, EX - 2, 8, 128), F32),
            inner, inner, thin, thin,
            pltpu.VMEM((2, 8, 128), F32),
            pltpu.VMEM((NZC - 1, 8, 128), F32),
            pltpu.VMEM((NGY - 1, 8, 128), F32),
            pltpu.VMEM((2, 128, 128), F32),
            pltpu.VMEM((2, NSRCG, 16, 128), F32),
            dma((2,)),
            dma((2, 3, 2, 3)), dma((2, 3, 2, 3)),
            dma((3, 2, 3)), dma((3, 2, 3)),
            dma((NSRCG - 1,)), dma((NSRCG - 1,)),
            dma((NZC - 1,)), dma((NZC - 1,)),
            dma((NGY - 1,)), dma((NGY - 1,)),
            dma((2, NSRCG)), dma((2, NSRCG)),
        ],
        compiler_params=pltpu.CompilerParams(
            collective_id=0, has_side_effects=True, vmem_limit_bytes=40 * 1024 * 1024
        ),
    )(warm_potential, warm_adjoint, turned, electrodes, receivers, observed, source_order)
    return result.T.reshape(xr, yr, depth)


def solution(mesh):
    in_specs = (
        P("src", "gx", "gy", None),
        P("src", "gx", "gy", None),
        P("gx", "gy", "src"),
        P(),
        P(),
        P(),
        P(),
    )
    out_specs = P("gx", "gy", "src")
    return jax.shard_map(body, mesh=mesh, in_specs=in_specs, out_specs=out_specs, check_vma=False)
```

```python
import functools

import jax
import jax.numpy as jnp
from jax import lax
from jax.experimental import pallas as pl
from jax.experimental.pallas import tpu as pltpu
from jax.sharding import PartitionSpec as P

MESH = pl.DeviceIdType.MESH
SWEEPS = 6
lowest = 0.05
highest = 2.0
centre = (highest + lowest) / 2.0
half_span = (highest - lowest) / 2.0
bound_ratio = centre / half_span
strength = 4.0

F32 = jnp.float32
I32 = jnp.int32
BF16 = jnp.bfloat16

NSRCG, NGX, NGY = 8, 16, 4
NZC = NGX // 2
NX, NY = 64, 128
XR, YR = 4, 32
CX = 2 * XR
HALO = 8
EX, EY = CX + 2 * HALO, YR + 2 * HALO


def chebyshev():
    out = []
    factor = 1.0 / bound_ratio
    for _ in range(SWEEPS):
        following = 1.0 / (2.0 * bound_ratio - factor)
        out.append((following * factor, 2.0 * following / half_span))
        factor = following
    return out


STEPS = chebyshev()
BLOCKS = {22: 11, 20: 5, 18: 6, 16: 4, 14: 7, 12: 6, 10: 5}


def split3(v):
    hi = v.astype(BF16)
    rest = v - hi.astype(F32)
    mid = rest.astype(BF16)
    lo = (rest - mid.astype(F32)).astype(BF16)
    return hi, mid, lo


def kernel(
    wp_ref, wa_ref, cond_hbm, elec_hbm, rec_hbm, obs_hbm, order_hbm,
    out_ref,
    cond_v, cond_ref, elec_ref, rec_v, obs_ref, order_ref,
    p0, p1, a0, a1, cext, coef, slope, gath, pan, pick, pick_own,
    scond, scoef, sinv, srhs, y0, y1, vm, zbuf, gbuf, gt, rbuf,
    loc_sem, warm_s, warm_r, cond_s, cond_r, src_s, src_r, z_s, z_r, g_s, g_r, rs_s, rs_r,
):
    src = lax.axis_index("src")
    gx = lax.axis_index("gx")
    gy = lax.axis_index("gy")
    zc = gx // 2
    core = gx - 2 * zc

    def place(ds=0, dz=0, t=0, dg=0):
        z2 = lax.rem(zc + (dz % NZC), NZC)
        c2 = core if t == 0 else 1 - core
        return {
            "src": lax.rem(src + (ds % NSRCG), NSRCG),
            "gx": 2 * z2 + c2,
            "gy": lax.rem(gy + (dg % NGY), NGY),
        }

    halo = [
        (dz, t, dg)
        for dg in (0, 1, -1)
        for dz in (0, 1, -1)
        for t in (1, 0)
        if (dz, t, dg) != (0, 0, 0)
    ]

    partners = [place(dz=dz, t=t, dg=dg) for dz, t, dg in halo]
    partners += [place(ds=ds, t=t) for ds in range(1, NSRCG) for t in (0, 1)]
    partners += [place(dz=dz) for dz in range(2, NZC - 1)]
    partners += [place(dg=dg) for dg in range(2, NGY - 1)]
    barrier = pltpu.get_barrier_semaphore()
    for device in partners:
        pl.semaphore_signal(barrier, inc=1, device_id=device, device_id_type=MESH)

    own_x = pl.ds(HALO + XR * core, XR)
    half = pl.ds(2 * core, 2)
    own_p = pltpu.make_async_copy(wp_ref.at[half], p0.at[:, own_x, HALO : HALO + YR, :], loc_sem.at[0])
    own_a = pltpu.make_async_copy(wa_ref.at[half], a0.at[:, own_x, HALO : HALO + YR, :], loc_sem.at[1])
    small = [
        pltpu.make_async_copy(a, b, loc_sem.at[2 + i])
        for i, (a, b) in enumerate(
            ((cond_hbm, cond_v), (rec_hbm, rec_v), (order_hbm, order_ref), (elec_hbm, elec_ref), (obs_hbm, obs_ref))
        )
    ]
    for copy in small:
        copy.start()
    own_p.start()
    own_a.start()
    for copy in small:
        copy.wait()

    own_rows = pl.ds(pl.multiple_of(16 * src, 16), 16)
    piece = jnp.concatenate([cond_v[x] for x in range(XR)], axis=1)
    cond_ref[...] = piece
    gath[own_rows, :] = piece

    pl.semaphore_wait(barrier, len(partners))

    gathers = [
        pltpu.make_async_remote_copy(
            cond_ref, gath.at[own_rows, :], src_s.at[ds - 1], src_r.at[ds - 1],
            device_id=place(ds=ds), device_id_type=MESH,
        )
        for ds in range(1, NSRCG)
    ]
    for copy in gathers:
        copy.start()

    def y_spans(dg):
        if dg == 0:
            return slice(0, YR), slice(HALO, HALO + YR)
        if dg == 1:
            return slice(YR - HALO, YR), slice(0, HALO)
        return slice(0, HALO), slice(HALO + YR, EY)

    def warm_copies(which, ref, dest):
        copies = []
        for dz, t, dg in halo:
            ys, yd = y_spans(dg)
            c2 = core if t == 0 else 1 - core
            copies.append(
                pltpu.make_async_remote_copy(
                    ref.at[pl.ds(2 * c2, 2), :, ys, :],
                    dest.at[:, pl.ds(HALO * (1 - dz) + XR * core, XR), yd, :],
                    warm_s.at[which, dz + 1, t, dg + 1],
                    warm_r.at[which, dz + 1, t, dg + 1],
                    device_id=place(dz=dz, t=t, dg=dg), device_id_type=MESH,
                )
            )
        return copies

    copies_p = warm_copies(0, wp_ref, p0)
    copies_a = warm_copies(1, wa_ref, a0)
    straight = [dz == 0 or dg == 0 for dz, t, dg in halo]
    for copy, now in zip(copies_p, straight):
        if now:
            copy.start()

    cells = jnp.concatenate([rec_v[...].astype(F32), jnp.zeros((126, 128), F32)], axis=0)
    cells = jnp.transpose(cells).astype(I32)
    rx0 = cells[:, 0:1] >> 7
    ry0 = cells[:, 0:1] & (NY - 1)
    rx1 = cells[:, 1:2] >> 7
    ry1 = cells[:, 1:2] & (NY - 1)

    def own_flat(cx, cy):
        lx = cx - CX * zc
        ly = cy - YR * gy
        inside = (lx >= 0) & (lx < CX) & (ly >= 0) & (ly < YR)
        return jnp.where(inside, lx * YR + ly, -1)

    flats = lax.broadcasted_iota(I32, (128, CX * YR), 1)
    pick_own[...] = (
        jnp.where(own_flat(rx0, ry0) == flats, 1.0, 0.0)
        - jnp.where(own_flat(rx1, ry1) == flats, 1.0, 0.0)
    ).astype(BF16)

    lanes = lax.broadcasted_iota(I32, (128, 128), 1)
    ylane = lanes & 63
    ycell = (YR * gy - HALO + ylane) & (NY - 1)
    ok0 = (ry0 == ycell) & (ylane < EY)
    ok1 = (ry1 == ycell) & (ylane < EY)
    col0 = jnp.where(ok0, rx0, -1)
    col1 = jnp.where(ok1, rx1, -1)
    for r in range(EX):
        xrow = (CX * zc - HALO + r) & (NX - 1)
        pick[:, r * 128 : (r + 1) * 128] = (
            jnp.where(col0 == xrow, 1.0, 0.0) - jnp.where(col1 == xrow, 1.0, 0.0)
        ).astype(BF16)

    for copy in gathers:
        copy.wait_recv()
    pan[...] = jnp.transpose(gath[...]).reshape(XR, YR, 128)
    cext[own_x, HALO : HALO + YR, :] = pan[...]
    copies_c = []
    for dz, t, dg in halo:
        ys, yd = y_spans(dg)
        copies_c.append(
            pltpu.make_async_remote_copy(
                pan.at[:, ys, :],
                cext.at[pl.ds(HALO * (1 - dz) + XR * core, XR), yd, :],
                cond_s.at[dz + 1, t, dg + 1],
                cond_r.at[dz + 1, t, dg + 1],
                device_id=place(dz=dz, t=t, dg=dg), device_id_type=MESH,
            )
        )
    for copy in copies_c:
        copy.start()
    for copy, now in zip(copies_p, straight):
        if not now:
            copy.start()
    for copy in copies_a:
        copy.start()
    for copy in copies_c:
        copy.wait_recv()

    yy = (YR * gy - HALO + lax.broadcasted_iota(I32, (EY, 128), 0)) & (NY - 1)
    zz = lax.broadcasted_iota(I32, (EY, 128), 1)
    in_ym = yy != 0
    in_yp = yy != NY - 1
    in_zm = zz != 0
    in_zp = zz != 127

    def x_inside(r):
        row = (CX * zc - HALO + r) & (NX - 1)
        return jnp.where(row == 0, 0.0, 1.0).astype(F32), jnp.where(row == NX - 1, 0.0, 1.0).astype(F32)

    def harmonic(s, n):
        return 2.0 * s * n / (s + n)

    def coef_row(r, carry):
        s = cext[r]
        fm, fp = x_inside(r)
        hxm = harmonic(s, cext[r - 1]) * fm
        hxp = harmonic(s, cext[r + 1]) * fp
        hym = jnp.where(in_ym, harmonic(s, pltpu.roll(s, 1, 0)), 0.0)
        hyp = jnp.where(in_yp, harmonic(s, pltpu.roll(s, EY - 1, 0)), 0.0)
        hzm = jnp.where(in_zm, harmonic(s, pltpu.roll(s, 1, 1)), 0.0)
        hzp = jnp.where(in_zp, harmonic(s, pltpu.roll(s, 127, 1)), 0.0)
        diag = hxm + hxp + hym + hyp + hzm + hzp
        diag = diag + s * ((1.0 - fm) + (1.0 - fp))
        diag = diag + jnp.where(in_ym, 0.0, s) + jnp.where(in_yp, 0.0, s) + jnp.where(in_zp, 0.0, s)
        inv = 1.0 / diag
        for i, h in enumerate((hxm, hxp, hym, hyp, hzm, hzp)):
            coef[i, r] = h * inv
        return carry

    lax.fori_loop(1, EX - 1, coef_row, 0, unroll=2)

    def slope_of(s, n):
        total = s + n
        return 2.0 * n * n / (total * total)

    def slope_row(r, carry):
        s = cext[r]
        fm, fp = x_inside(r)
        q = r - HALO
        slope[0, q] = slope_of(s, cext[r - 1]) * fm + (1.0 - fm)
        slope[1, q] = slope_of(s, cext[r + 1]) * fp + (1.0 - fp)
        slope[2, q] = jnp.where(in_ym, slope_of(s, pltpu.roll(s, 1, 0)), 1.0)
        slope[3, q] = jnp.where(in_yp, slope_of(s, pltpu.roll(s, EY - 1, 0)), 1.0)
        slope[4, q] = jnp.where(in_zm, slope_of(s, pltpu.roll(s, 1, 1)), 0.0)
        slope[5, q] = jnp.where(in_zp, slope_of(s, pltpu.roll(s, 127, 1)), 1.0)
        return carry

    for first, count in ((0, 16), (16, 8)):
        gathered = jnp.ones((EY, 128), F32)
        for i in range(count):
            rolled = pltpu.roll(cext[first + i], 8 * i, 1) if i else cext[first]
            gathered = jnp.where((zz >= 8 * i) & (zz < 8 * i + 8), rolled, gathered)
        ones = jnp.ones((64 - EY, 128), F32)
        turned = jnp.transpose(jnp.concatenate([gathered, ones, gathered, ones], axis=0))
        scond[first : first + count] = turned[: 8 * count].reshape(count, 8, 128)

    shape = (EX - 2, 8, 128)
    lane3 = lax.broadcasted_iota(I32, shape, 2)
    sub3 = lax.broadcasted_iota(I32, shape, 1)
    row3 = (lax.broadcasted_iota(I32, shape, 0) + (CX * zc - HALO + 1)) & (NX - 1)
    y3 = (YR * gy - HALO + (lane3 & 63)) & (NY - 1)
    s = scond[1 : EX - 1]
    hs = [
        (harmonic(s, scond[0 : EX - 2]), row3 != 0, True),
        (harmonic(s, scond[2:EX]), row3 != NX - 1, True),
        (harmonic(s, pltpu.roll(s, 1, 2)), y3 != 0, True),
        (harmonic(s, pltpu.roll(s, 127, 2)), y3 != NY - 1, True),
        (harmonic(s, pltpu.roll(s, 1, 1)), sub3 != 0, False),
        (harmonic(s, pltpu.roll(s, 7, 1)), sub3 != 7, False),
    ]
    diag = jnp.zeros(shape, F32)
    for h, inside, outer in hs:
        diag = diag + jnp.where(inside, h, s if outer else 0.0)
    inv = 1.0 / diag
    sinv[...] = inv
    for i, (h, inside, outer) in enumerate(hs):
        scoef[i] = jnp.where(inside, h, 0.0) * inv

    def thin_solve():
        g = sinv[...] * srhs[...]
        zero = jnp.zeros((1, 8, 128), F32)
        for ref in (y0, y1):
            ref[0:1] = zero
            ref[EX - 1 : EX] = zero
        y0[1 : EX - 1] = jnp.zeros(shape, F32)
        y1[1 : EX - 1] = g * (1.0 / centre)
        older, newer = y0, y1
        for a, b in STEPS:
            u = newer[1 : EX - 1]
            total = scoef[0] * newer[0 : EX - 2] + scoef[1] * newer[2:EX]
            total = total + scoef[2] * pltpu.roll(u, 1, 2) + scoef[3] * pltpu.roll(u, 127, 2)
            total = total + scoef[4] * pltpu.roll(u, 1, 1) + scoef[5] * pltpu.roll(u, 7, 1)
            older[1 : EX - 1] = (1.0 + a - b) * u - a * older[1 : EX - 1] + b * (sinv[...] * srhs[...] + total)
            older, newer = newer, older
        return newer

    def add_thin(thin, dest):
        first = HALO - 1
        turned = jnp.transpose(thin[first : first + 16].reshape(128, 128))
        shallow = lanes < 8
        for i in range(CX + 2):
            part = jnp.where(shallow, pltpu.roll(turned, (128 - 8 * i) % 128, 1) if i else turned, 0.0)
            for slot in range(2):
                dest[slot, first + i] = dest[slot, first + i] + part[64 * slot : 64 * slot + EY]

    first_slot = 4 * src + 2 * core
    idents = [order_ref[first_slot + j] for j in range(2)]
    rhs = jnp.zeros(shape, F32)
    for e, sign in ((0, strength), (1, -strength)):
        cells = [elec_ref[e, k] for k in idents]
        ex = jnp.where(lane3 < 64, cells[0] >> 7, cells[1] >> 7)
        ey = jnp.where(lane3 < 64, cells[0] & (NY - 1), cells[1] & (NY - 1))
        hit = (ex == row3) & (ey == y3) & (sub3 == 0) & ((lane3 & 63) < EY)
        rhs = rhs + jnp.where(hit, sign, 0.0)
    srhs[...] = rhs
    thin_p = thin_solve()

    def app(x, prev, dest, wc, wu, wp, e):
        rows = CX + 2 * e
        block = BLOCKS[rows]

        def step(q, carry):
            fresh = []
            for i in range(block):
                r = HALO - e + q * block + i
                c = [coef[j, r] for j in range(6)]
                for slot in range(2):
                    u = x[slot, r]
                    total = c[0] * x[slot, r - 1] + c[1] * x[slot, r + 1]
                    total = total + c[2] * pltpu.roll(u, 1, 0) + c[3] * pltpu.roll(u, EY - 1, 0)
                    total = total + c[4] * pltpu.roll(u, 1, 1) + c[5] * pltpu.roll(u, 127, 1)
                    value = wu * u + wc * total
                    if prev is not None:
                        value = value - wp * prev[slot, r]
                    fresh.append((slot, r, value))
            for slot, r, value in fresh:
                dest[slot, r] = value
            return carry

        lax.fori_loop(0, rows // block, step, 0)

    def full_solve(x0, x1, first, last):
        if first == 0:
            app(x0, None, x1, 1.0 / centre, 1.0 - 1.0 / centre, 0.0, HALO - 1)
        for k in range(max(first, 1), last):
            a, b = STEPS[k - 1]
            older, newer = (x0, x1) if k % 2 else (x1, x0)
            app(newer, older, older, b, 1.0 + a - b, a, HALO - 1 - k)
        return x1

    own_p.wait()
    for copy in copies_p:
        copy.wait_recv()
    pot = full_solve(p0, p1, 0, SWEEPS + 1)
    add_thin(thin_p, pot)

    value = jnp.zeros((128, 128), F32)
    for slot in range(2):
        block = pot[slot, HALO : HALO + CX, HALO : HALO + YR, :].reshape(CX * YR, 128)
        got = jnp.zeros((128, 128), F32)
        for part in split3(block):
            got = got + jnp.dot(pick_own[...], part, preferred_element_type=F32)
        if slot:
            got = pltpu.roll(got, slot, 1)
        value = jnp.where(lanes == slot, got, value)
    vm[0] = jnp.transpose(value)[0:8]
    copies_z = [
        pltpu.make_async_remote_copy(
            vm.at[0], zbuf.at[dz - 1], z_s.at[dz - 1], z_r.at[dz - 1],
            device_id=place(dz=dz), device_id_type=MESH,
        )
        for dz in range(1, NZC)
    ]
    for copy in copies_z:
        copy.start()

    own_a.wait()
    for copy in copies_a:
        copy.wait_recv()
    full_solve(a0, a1, 0, 4)

    for copy in copies_z:
        copy.wait_recv()
    total = vm[0]
    for i in range(NZC - 1):
        total = total + zbuf[i]
    vm[1] = total
    copies_g = [
        pltpu.make_async_remote_copy(
            vm.at[1], gbuf.at[dg - 1], g_s.at[dg - 1], g_r.at[dg - 1],
            device_id=place(dg=dg), device_id_type=MESH,
        )
        for dg in range(1, NGY)
    ]
    for copy in copies_g:
        copy.start()

    adj = full_solve(a0, a1, 4, SWEEPS + 1)
    lax.fori_loop(HALO, HALO + CX, slope_row, 0, unroll=2)

    for copy in copies_g:
        copy.wait_recv()
    total = vm[1]
    for i in range(NGY - 1):
        total = total + gbuf[i]
    sub8 = lax.broadcasted_iota(I32, (8, 128), 0)
    lane8 = lax.broadcasted_iota(I32, (8, 128), 1)
    seen = jnp.where(sub8 == 0, obs_ref[pl.ds(idents[0], 1), :], obs_ref[pl.ds(idents[1], 1), :])
    misfit = jnp.where(sub8 < 2, total - seen, 0.0)
    hi, mid, lo = split3(misfit)
    stacked = jnp.concatenate(
        [hi.astype(F32), mid.astype(F32), lo.astype(F32), jnp.zeros((8, 128), F32)], axis=0
    ).astype(BF16)
    back = jnp.dot(stacked, pick[...], preferred_element_type=F32)
    for r in range(1, EX - 1):
        cut = back[:, r * 128 : (r + 1) * 128]
        both = cut[0:8] + cut[8:16] + cut[16:24]
        line = jnp.where(lane8[0:1] < 64, both[0:1], both[1:2])
        srhs[r - 1] = jnp.where(sub8 == 0, line, 0.0)
    add_thin(thin_solve(), adj)

    def grad_row(r, carry):
        q = r - HALO
        fm, fp = x_inside(r)
        sums = [jnp.zeros((EY, 128), F32) for _ in range(6)]
        for slot in range(2):
            p = pot[slot, r]
            a = adj[slot, r]
            near = [
                (pot[slot, r - 1] * fm, adj[slot, r - 1] * fm),
                (pot[slot, r + 1] * fp, adj[slot, r + 1] * fp),
            ]
            for inside, shift, axis in ((in_ym, 1, 0), (in_yp, EY - 1, 0), (in_zm, 1, 1), (in_zp, 127, 1)):
                near.append(
                    (
                        jnp.where(inside, pltpu.roll(p, shift, axis), 0.0),
                        jnp.where(inside, pltpu.roll(a, shift, axis), 0.0),
                    )
                )
            sums = [old + (p - pn) * (a - an) for old, (pn, an) in zip(sums, near)]
        out = slope[0, q] * sums[0]
        for i in range(1, 6):
            out = out + slope[i, q] * sums[i]
        pan8[q] = out[HALO : HALO + YR]
        return carry

    pan8 = slope.at[0, :, 0:YR, :]

    lax.fori_loop(HALO, HALO + CX, grad_row, 0, unroll=2)
    for c in range(2):
        gt[c] = jnp.transpose(slope[0, XR * c : XR * c + XR, 0:YR, :].reshape(128, 128))

    def rs_copy(ds, t):
        c2 = core if t == 0 else 1 - core
        s2 = lax.rem(src + ds, NSRCG)
        return pltpu.make_async_remote_copy(
            gt.at[c2, pl.ds(pl.multiple_of(16 * s2, 16), 16), :],
            rbuf.at[t, ds],
            rs_s.at[t, ds], rs_r.at[t, ds],
            device_id=place(ds=ds, t=t), device_id_type=MESH,
        )

    copies_rs = [rs_copy(ds, t) for ds in range(NSRCG) for t in (0, 1) if ds or t]
    for copy in copies_rs:
        copy.start()
    for copy in copies_rs:
        copy.wait_recv()
    total = gt[core, own_rows, :]
    for ds in range(NSRCG):
        for t in (0, 1):
            if ds or t:
                total = total + rbuf[t, ds]
    total = -total
    for x in range(XR):
        out_ref[x] = (pltpu.roll(total, 128 - YR * x, 1) if x else total)[:, :YR]

    for copies in (gathers, copies_p, copies_a, copies_c, copies_z, copies_g, copies_rs):
        for copy in copies:
            copy.wait_send()


def body(warm_potential, warm_adjoint, conductivity, electrodes, receivers, observed, source_order):
    xr, yr, depth = conductivity.shape
    hbm = pl.BlockSpec(memory_space=pltpu.HBM)
    vmem = pl.BlockSpec(memory_space=pltpu.VMEM)
    field = pltpu.VMEM((2, EX, EY, 128), F32)
    thin = pltpu.VMEM((EX, 8, 128), F32)
    inner = pltpu.VMEM((EX - 2, 8, 128), F32)
    dma = pltpu.SemaphoreType.DMA
    result = pl.pallas_call(
        kernel,
        out_shape=jax.ShapeDtypeStruct((xr, depth, yr), F32),
        in_specs=[hbm] * 7,
        out_specs=vmem,
        scratch_shapes=[
            pltpu.VMEM((xr, depth, yr), F32),
            pltpu.VMEM((depth, xr * yr), F32),
            pltpu.SMEM((2, 32), I32),
            pltpu.VMEM((2, 128), I32),
            pltpu.VMEM((32, 128), F32),
            pltpu.SMEM((32,), I32),
            field, field, field, field,
            pltpu.VMEM((EX, EY, 128), F32),
            pltpu.VMEM((6, EX, EY, 128), F32),
            pltpu.VMEM((6, CX, EY, 128), F32),
            pltpu.VMEM((128, 128), F32),
            pltpu.VMEM((XR, YR, 128), F32),
            pltpu.VMEM((128, EX * 128), BF16),
            pltpu.VMEM((128, CX * YR), BF16),
            thin,
            pltpu.VMEM((6, EX - 2, 8, 128), F32),
            inner, inner, thin, thin,
            pltpu.VMEM((2, 8, 128), F32),
            pltpu.VMEM((NZC - 1, 8, 128), F32),
            pltpu.VMEM((NGY - 1, 8, 128), F32),
            pltpu.VMEM((2, 128, 128), F32),
            pltpu.VMEM((2, NSRCG, 16, 128), F32),
            dma((7,)),
            dma((2, 3, 2, 3)), dma((2, 3, 2, 3)),
            dma((3, 2, 3)), dma((3, 2, 3)),
            dma((NSRCG - 1,)), dma((NSRCG - 1,)),
            dma((NZC - 1,)), dma((NZC - 1,)),
            dma((NGY - 1,)), dma((NGY - 1,)),
            dma((2, NSRCG)), dma((2, NSRCG)),
        ],
        compiler_params=pltpu.CompilerParams(
            collective_id=0, has_side_effects=True, vmem_limit_bytes=63 * 1024 * 1024
        ),
    )(
        warm_potential, warm_adjoint, jnp.transpose(conductivity, (0, 2, 1)), electrodes.T, receivers.T,
        observed, source_order,
    )
    return jnp.transpose(result, (0, 2, 1))


def solution(mesh):
    in_specs = (
        P("src", "gx", "gy", None),
        P("src", "gx", "gy", None),
        P("gx", "gy", "src"),
        P(),
        P(),
        P(),
        P(),
    )
    out_specs = P("gx", "gy", "src")
    return jax.shard_map(body, mesh=mesh, in_specs=in_specs, out_specs=out_specs, check_vma=False)
```

```python
import functools

import jax
import jax.numpy as jnp
from jax import lax
from jax.experimental import pallas as pl
from jax.experimental.pallas import tpu as pltpu
from jax.sharding import PartitionSpec as P

MESH = pl.DeviceIdType.MESH
SWEEPS = 6
lowest = 0.05
highest = 2.0
centre = (highest + lowest) / 2.0
half_span = (highest - lowest) / 2.0
bound_ratio = centre / half_span
strength = 4.0

F32 = jnp.float32
I32 = jnp.int32
BF16 = jnp.bfloat16

NSRCG, NGX, NGY = 8, 16, 4
NZC = NGX // 2
NX, NY = 64, 128
XR, YR = 4, 32
CX = 2 * XR
HALO = 8
EX, EY = CX + 2 * HALO, YR + 2 * HALO


def chebyshev():
    out = []
    factor = 1.0 / bound_ratio
    for _ in range(SWEEPS):
        following = 1.0 / (2.0 * bound_ratio - factor)
        out.append((following * factor, 2.0 * following / half_span))
        factor = following
    return out


STEPS = chebyshev()
BLOCKS = {22: 11, 20: 10, 18: 9, 16: 8, 14: 7, 12: 12, 10: 10}


def split3(v):
    hi = v.astype(BF16)
    rest = v - hi.astype(F32)
    mid = rest.astype(BF16)
    lo = (rest - mid.astype(F32)).astype(BF16)
    return hi, mid, lo


def kernel(
    wp_ref, wa_ref, cond_hbm, elec_hbm, rec_hbm, obs_hbm, order_hbm,
    out_ref,
    cond_v, cond_ref, elec_ref, rec_v, obs_ref, order_ref,
    p0, p1, a0, a1, cext, coef, slope, gath, pan, pick, pick_own,
    scond, scoef, sinv, srhs, y0, y1, vm, zbuf, gbuf, gt, rbuf,
    loc_sem, warm_s, warm_r, cond_s, cond_r, src_s, src_r, z_s, z_r, g_s, g_r, rs_s, rs_r,
):
    src = lax.axis_index("src")
    gx = lax.axis_index("gx")
    gy = lax.axis_index("gy")
    zc = gx // 2
    core = gx - 2 * zc

    def place(ds=0, dz=0, t=0, dg=0):
        z2 = lax.rem(zc + (dz % NZC), NZC)
        c2 = core if t == 0 else 1 - core
        return {
            "src": lax.rem(src + (ds % NSRCG), NSRCG),
            "gx": 2 * z2 + c2,
            "gy": lax.rem(gy + (dg % NGY), NGY),
        }

    halo = [
        (dz, t, dg)
        for dg in (0, 1, -1)
        for dz in (0, 1, -1)
        for t in (1, 0)
        if (dz, t, dg) != (0, 0, 0)
    ]

    partners = [place(dz=dz, t=t, dg=dg) for dz, t, dg in halo]
    partners += [place(ds=ds, t=t) for ds in range(1, NSRCG) for t in (0, 1)]
    partners += [place(dz=dz) for dz in range(2, NZC - 1)]
    partners += [place(dg=dg) for dg in range(2, NGY - 1)]
    barrier = pltpu.get_barrier_semaphore()
    for device in partners:
        pl.semaphore_signal(barrier, inc=1, device_id=device, device_id_type=MESH)

    own_x = pl.ds(HALO + XR * core, XR)
    def settle(ref, sem):
        pltpu.make_async_copy(ref, ref, sem).wait()

    owns = [
        pltpu.make_async_copy(
            ref.at[2 * core + slot], dest.at[slot, own_x, HALO : HALO + YR, :], warm_r.at[which, slot]
        )
        for which, (ref, dest) in enumerate(((wp_ref, p0), (wa_ref, a0)))
        for slot in range(2)
    ]
    small = [
        pltpu.make_async_copy(a, b, loc_sem.at[i])
        for i, (a, b) in enumerate(
            ((cond_hbm, cond_v), (rec_hbm, rec_v), (order_hbm, order_ref), (elec_hbm, elec_ref), (obs_hbm, obs_ref))
        )
    ]
    for copy in small:
        copy.start()
    for copy in owns:
        copy.start()
    for copy in small:
        copy.wait()

    own_rows = pl.ds(pl.multiple_of(16 * src, 16), 16)
    piece = jnp.concatenate([cond_v[x] for x in range(XR)], axis=1)
    cond_ref[...] = piece
    pltpu.make_async_copy(cond_ref, gath.at[own_rows, :], src_r).start()

    pl.semaphore_wait(barrier, len(partners))

    gathers = [
        pltpu.make_async_remote_copy(
            cond_ref, gath.at[own_rows, :], src_s, src_r,
            device_id=place(ds=ds), device_id_type=MESH,
        )
        for ds in range(1, NSRCG)
    ]
    for copy in gathers:
        copy.start()

    def y_spans(dg):
        if dg == 0:
            return slice(0, YR), slice(HALO, HALO + YR)
        if dg == 1:
            return slice(YR - HALO, YR), slice(0, HALO)
        return slice(0, HALO), slice(HALO + YR, EY)

    def warm_copies(which, ref, dest, slot):
        copies = []
        for dz, t, dg in halo:
            ys, yd = y_spans(dg)
            c2 = core if t == 0 else 1 - core
            copies.append(
                pltpu.make_async_remote_copy(
                    ref.at[2 * c2 + slot, :, ys, :],
                    dest.at[slot, pl.ds(HALO * (1 - dz) + XR * core, XR), yd, :],
                    warm_s.at[which, slot], warm_r.at[which, slot],
                    device_id=place(dz=dz, t=t, dg=dg), device_id_type=MESH,
                )
            )
        return copies

    copies_p = [warm_copies(0, wp_ref, p0, slot) for slot in range(2)]
    copies_a = [warm_copies(1, wa_ref, a0, slot) for slot in range(2)]
    for copy in copies_p[0]:
        copy.start()

    cells = jnp.concatenate([rec_v[...].astype(F32), jnp.zeros((126, 128), F32)], axis=0)
    cells = jnp.transpose(cells).astype(I32)
    rx0 = cells[:, 0:1] >> 7
    ry0 = cells[:, 0:1] & (NY - 1)
    rx1 = cells[:, 1:2] >> 7
    ry1 = cells[:, 1:2] & (NY - 1)

    def own_flat(cx, cy):
        lx = cx - CX * zc
        ly = cy - YR * gy
        inside = (lx >= 0) & (lx < CX) & (ly >= 0) & (ly < YR)
        return jnp.where(inside, lx * YR + ly, -1)

    flats = lax.broadcasted_iota(I32, (128, CX * YR), 1)
    pick_own[...] = (
        jnp.where(own_flat(rx0, ry0) == flats, 1.0, 0.0)
        - jnp.where(own_flat(rx1, ry1) == flats, 1.0, 0.0)
    ).astype(BF16)

    lanes = lax.broadcasted_iota(I32, (128, 128), 1)
    ylane = lanes & 63
    ycell = (YR * gy - HALO + ylane) & (NY - 1)
    ok0 = (ry0 == ycell) & (ylane < EY)
    ok1 = (ry1 == ycell) & (ylane < EY)
    col0 = jnp.where(ok0, rx0, -1)
    col1 = jnp.where(ok1, rx1, -1)
    for r in range(EX):
        xrow = (CX * zc - HALO + r) & (NX - 1)
        pick[:, r * 128 : (r + 1) * 128] = (
            jnp.where(col0 == xrow, 1.0, 0.0) - jnp.where(col1 == xrow, 1.0, 0.0)
        ).astype(BF16)

    settle(gath, src_r)
    pan[...] = jnp.transpose(gath[...]).reshape(XR, YR, 128)
    pltpu.make_async_copy(pan, cext.at[own_x, HALO : HALO + YR, :], cond_r).start()
    copies_c = []
    for dz, t, dg in halo:
        ys, yd = y_spans(dg)
        copies_c.append(
            pltpu.make_async_remote_copy(
                pan.at[:, ys, :],
                cext.at[pl.ds(HALO * (1 - dz) + XR * core, XR), yd, :],
                cond_s, cond_r,
                device_id=place(dz=dz, t=t, dg=dg), device_id_type=MESH,
            )
        )
    for copy in copies_c:
        copy.start()
    for copy in copies_p[1]:
        copy.start()
    settle(cext, cond_r)
    for copy in copies_a[0]:
        copy.start()

    yy = (YR * gy - HALO + lax.broadcasted_iota(I32, (EY, 128), 0)) & (NY - 1)
    zz = lax.broadcasted_iota(I32, (EY, 128), 1)
    in_ym = yy != 0
    in_yp = yy != NY - 1
    in_zm = zz != 0
    in_zp = zz != 127

    def x_inside(r):
        row = (CX * zc - HALO + r) & (NX - 1)
        return jnp.where(row == 0, 0.0, 1.0).astype(F32), jnp.where(row == NX - 1, 0.0, 1.0).astype(F32)

    def harmonic(s, n):
        return 2.0 * s * n / (s + n)

    def coef_row(r, carry):
        s = cext[r]
        fm, fp = x_inside(r)
        hxm = harmonic(s, cext[r - 1]) * fm
        hxp = harmonic(s, cext[r + 1]) * fp
        hym = jnp.where(in_ym, harmonic(s, pltpu.roll(s, 1, 0)), 0.0)
        hyp = jnp.where(in_yp, harmonic(s, pltpu.roll(s, EY - 1, 0)), 0.0)
        hzm = jnp.where(in_zm, harmonic(s, pltpu.roll(s, 1, 1)), 0.0)
        hzp = jnp.where(in_zp, harmonic(s, pltpu.roll(s, 127, 1)), 0.0)
        diag = hxm + hxp + hym + hyp + hzm + hzp
        diag = diag + s * ((1.0 - fm) + (1.0 - fp))
        diag = diag + jnp.where(in_ym, 0.0, s) + jnp.where(in_yp, 0.0, s) + jnp.where(in_zp, 0.0, s)
        inv = 1.0 / diag
        for i, h in enumerate((hxm, hxp, hym, hyp, hzm, hzp)):
            coef[i, r] = h * inv
        return carry

    lax.fori_loop(1, EX - 1, coef_row, 0, unroll=2)

    def slope_of(s, n):
        total = s + n
        return 2.0 * n * n / (total * total)

    def slope_row(r, carry):
        s = cext[r]
        fm, fp = x_inside(r)
        q = r - HALO
        slope[0, q] = slope_of(s, cext[r - 1]) * fm + (1.0 - fm)
        slope[1, q] = slope_of(s, cext[r + 1]) * fp + (1.0 - fp)
        slope[2, q] = jnp.where(in_ym, slope_of(s, pltpu.roll(s, 1, 0)), 1.0)
        slope[3, q] = jnp.where(in_yp, slope_of(s, pltpu.roll(s, EY - 1, 0)), 1.0)
        slope[4, q] = jnp.where(in_zm, slope_of(s, pltpu.roll(s, 1, 1)), 0.0)
        slope[5, q] = jnp.where(in_zp, slope_of(s, pltpu.roll(s, 127, 1)), 1.0)
        return carry

    def app(slot, x, prev, dest, wc, wu, wp, e):
        rows = CX + 2 * e
        block = BLOCKS[rows]

        def step(q, carry):
            fresh = []
            for i in range(block):
                r = HALO - e + q * block + i
                u = x[slot, r]
                total = coef[0, r] * x[slot, r - 1] + coef[1, r] * x[slot, r + 1]
                total = total + coef[2, r] * pltpu.roll(u, 1, 0) + coef[3, r] * pltpu.roll(u, EY - 1, 0)
                total = total + coef[4, r] * pltpu.roll(u, 1, 1) + coef[5, r] * pltpu.roll(u, 127, 1)
                value = wu * u + wc * total
                if prev is not None:
                    value = value - wp * prev[slot, r]
                fresh.append((r, value))
            for r, value in fresh:
                dest[slot, r] = value
            return carry

        lax.fori_loop(0, rows // block, step, 0)

    def full_solve(which, slot, x0, x1):
        settle(x0.at[slot], warm_r.at[which, slot])
        app(slot, x0, None, x1, 1.0 / centre, 1.0 - 1.0 / centre, 0.0, HALO - 1)
        for k, (a, b) in enumerate(STEPS):
            older, newer = (x1, x0) if k % 2 else (x0, x1)
            app(slot, newer, older, older, b, 1.0 + a - b, a, HALO - 2 - k)

    pot, adj = p1, a1
    full_solve(0, 0, p0, p1)

    for first, count in ((0, 16), (16, 8)):
        gathered = jnp.ones((EY, 128), F32)
        for i in range(count):
            rolled = pltpu.roll(cext[first + i], 8 * i, 1) if i else cext[first]
            gathered = jnp.where((zz >= 8 * i) & (zz < 8 * i + 8), rolled, gathered)
        ones = jnp.ones((64 - EY, 128), F32)
        turned = jnp.transpose(jnp.concatenate([gathered, ones, gathered, ones], axis=0))
        scond[first : first + count] = turned[: 8 * count].reshape(count, 8, 128)

    shape = (EX - 2, 8, 128)
    lane3 = lax.broadcasted_iota(I32, shape, 2)
    sub3 = lax.broadcasted_iota(I32, shape, 1)
    row3 = (lax.broadcasted_iota(I32, shape, 0) + (CX * zc - HALO + 1)) & (NX - 1)
    y3 = (YR * gy - HALO + (lane3 & 63)) & (NY - 1)
    s = scond[1 : EX - 1]
    hs = [
        (harmonic(s, scond[0 : EX - 2]), row3 != 0, True),
        (harmonic(s, scond[2:EX]), row3 != NX - 1, True),
        (harmonic(s, pltpu.roll(s, 1, 2)), y3 != 0, True),
        (harmonic(s, pltpu.roll(s, 127, 2)), y3 != NY - 1, True),
        (harmonic(s, pltpu.roll(s, 1, 1)), sub3 != 0, False),
        (harmonic(s, pltpu.roll(s, 7, 1)), sub3 != 7, False),
    ]
    diag = jnp.zeros(shape, F32)
    for h, inside, outer in hs:
        diag = diag + jnp.where(inside, h, s if outer else 0.0)
    inv = 1.0 / diag
    sinv[...] = inv
    for i, (h, inside, outer) in enumerate(hs):
        scoef[i] = jnp.where(inside, h, 0.0) * inv

    def thin_solve():
        g = sinv[...] * srhs[...]
        zero = jnp.zeros((1, 8, 128), F32)
        for ref in (y0, y1):
            ref[0:1] = zero
            ref[EX - 1 : EX] = zero
        y0[1 : EX - 1] = jnp.zeros(shape, F32)
        y1[1 : EX - 1] = g * (1.0 / centre)
        older, newer = y0, y1
        for a, b in STEPS:
            u = newer[1 : EX - 1]
            total = scoef[0] * newer[0 : EX - 2] + scoef[1] * newer[2:EX]
            total = total + scoef[2] * pltpu.roll(u, 1, 2) + scoef[3] * pltpu.roll(u, 127, 2)
            total = total + scoef[4] * pltpu.roll(u, 1, 1) + scoef[5] * pltpu.roll(u, 7, 1)
            older[1 : EX - 1] = (1.0 + a - b) * u - a * older[1 : EX - 1] + b * (sinv[...] * srhs[...] + total)
            older, newer = newer, older
        return newer

    def add_thin(thin, dest):
        first = HALO - 1
        turned = jnp.transpose(thin[first : first + 16].reshape(128, 128))
        shallow = lanes < 8
        for i in range(CX + 2):
            part = jnp.where(shallow, pltpu.roll(turned, (128 - 8 * i) % 128, 1) if i else turned, 0.0)
            for slot in range(2):
                dest[slot, first + i] = dest[slot, first + i] + part[64 * slot : 64 * slot + EY]

    first_slot = 4 * src + 2 * core
    idents = [order_ref[first_slot + j] for j in range(2)]
    rhs = jnp.zeros(shape, F32)
    for e, sign in ((0, strength), (1, -strength)):
        cells = [elec_ref[e, k] for k in idents]
        ex = jnp.where(lane3 < 64, cells[0] >> 7, cells[1] >> 7)
        ey = jnp.where(lane3 < 64, cells[0] & (NY - 1), cells[1] & (NY - 1))
        hit = (ex == row3) & (ey == y3) & (sub3 == 0) & ((lane3 & 63) < EY)
        rhs = rhs + jnp.where(hit, sign, 0.0)
    srhs[...] = rhs
    thin_p = thin_solve()

    for copy in copies_a[1]:
        copy.start()
    full_solve(0, 1, p0, p1)
    add_thin(thin_p, pot)

    value = jnp.zeros((128, 128), F32)
    for slot in range(2):
        block = pot[slot, HALO : HALO + CX, HALO : HALO + YR, :].reshape(CX * YR, 128)
        got = jnp.zeros((128, 128), F32)
        for part in split3(block):
            got = got + jnp.dot(pick_own[...], part, preferred_element_type=F32)
        if slot:
            got = pltpu.roll(got, slot, 1)
        value = jnp.where(lanes == slot, got, value)
    vm[0] = jnp.transpose(value)[0:8]
    copies_z = [
        pltpu.make_async_remote_copy(
            vm.at[0], zbuf.at[dz - 1], z_s, z_r,
            device_id=place(dz=dz), device_id_type=MESH,
        )
        for dz in range(1, NZC)
    ]
    for copy in copies_z:
        copy.start()

    lax.fori_loop(HALO, HALO + CX, slope_row, 0, unroll=2)
    full_solve(1, 0, a0, a1)

    settle(zbuf, z_r)
    total = vm[0]
    for i in range(NZC - 1):
        total = total + zbuf[i]
    vm[1] = total
    copies_g = [
        pltpu.make_async_remote_copy(
            vm.at[1], gbuf.at[dg - 1], g_s, g_r,
            device_id=place(dg=dg), device_id_type=MESH,
        )
        for dg in range(1, NGY)
    ]
    for copy in copies_g:
        copy.start()

    full_solve(1, 1, a0, a1)


    settle(gbuf, g_r)
    total = vm[1]
    for i in range(NGY - 1):
        total = total + gbuf[i]
    sub8 = lax.broadcasted_iota(I32, (8, 128), 0)
    lane8 = lax.broadcasted_iota(I32, (8, 128), 1)
    seen = jnp.where(sub8 == 0, obs_ref[pl.ds(idents[0], 1), :], obs_ref[pl.ds(idents[1], 1), :])
    misfit = jnp.where(sub8 < 2, total - seen, 0.0)
    hi, mid, lo = split3(misfit)
    stacked = jnp.concatenate(
        [hi.astype(F32), mid.astype(F32), lo.astype(F32), jnp.zeros((8, 128), F32)], axis=0
    ).astype(BF16)
    back = jnp.dot(stacked, pick[...], preferred_element_type=F32)
    for r in range(1, EX - 1):
        cut = back[:, r * 128 : (r + 1) * 128]
        both = cut[0:8] + cut[8:16] + cut[16:24]
        line = jnp.where(lane8[0:1] < 64, both[0:1], both[1:2])
        srhs[r - 1] = jnp.where(sub8 == 0, line, 0.0)
    add_thin(thin_solve(), adj)

    def grad_row(r, carry):
        q = r - HALO
        fm, fp = x_inside(r)
        sums = [jnp.zeros((EY, 128), F32) for _ in range(6)]
        for slot in range(2):
            p = pot[slot, r]
            a = adj[slot, r]
            near = [
                (pot[slot, r - 1] * fm, adj[slot, r - 1] * fm),
                (pot[slot, r + 1] * fp, adj[slot, r + 1] * fp),
            ]
            for inside, shift, axis in ((in_ym, 1, 0), (in_yp, EY - 1, 0), (in_zm, 1, 1), (in_zp, 127, 1)):
                near.append(
                    (
                        jnp.where(inside, pltpu.roll(p, shift, axis), 0.0),
                        jnp.where(inside, pltpu.roll(a, shift, axis), 0.0),
                    )
                )
            sums = [old + (p - pn) * (a - an) for old, (pn, an) in zip(sums, near)]
        out = slope[0, q] * sums[0]
        for i in range(1, 6):
            out = out + slope[i, q] * sums[i]
        pan8[q] = out[HALO : HALO + YR]
        return carry

    pan8 = slope.at[0, :, 0:YR, :]

    lax.fori_loop(HALO, HALO + CX, grad_row, 0, unroll=2)
    for c in range(2):
        gt[c] = jnp.transpose(slope[0, XR * c : XR * c + XR, 0:YR, :].reshape(128, 128))

    def rs_copy(ds, t):
        c2 = core if t == 0 else 1 - core
        s2 = lax.rem(src + ds, NSRCG)
        return pltpu.make_async_remote_copy(
            gt.at[c2, pl.ds(pl.multiple_of(16 * s2, 16), 16), :],
            rbuf.at[t, ds],
            rs_s, rs_r,
            device_id=place(ds=ds, t=t), device_id_type=MESH,
        )

    copies_rs = [rs_copy(ds, t) for ds in range(NSRCG) for t in (0, 1) if ds or t]
    for copy in copies_rs:
        copy.start()
    pltpu.make_async_copy(gt.at[core, own_rows, :], rbuf.at[0, 0], rs_r).start()
    settle(rbuf, rs_r)
    total = rbuf[0, 0] + rbuf[1, 0]
    for ds in range(1, NSRCG):
        total = total + (rbuf[0, ds] + rbuf[1, ds])
    total = -total
    for x in range(XR):
        out_ref[x] = (pltpu.roll(total, 128 - YR * x, 1) if x else total)[:, :YR]

    sent = p0.at[:, 0:16, 0:YR, :]
    for which in range(2):
        for slot in range(2):
            settle(sent, warm_s.at[which, slot])
    settle(sent, cond_s)
    settle(gath.at[0 : 16 * (NSRCG - 1), :], src_s)
    settle(zbuf, z_s)
    settle(gbuf, g_s)
    settle(gt.at[:, 0 : 8 * (2 * NSRCG - 1), :], rs_s)


def body(warm_potential, warm_adjoint, conductivity, electrodes, receivers, observed, source_order):
    xr, yr, depth = conductivity.shape
    hbm = pl.BlockSpec(memory_space=pltpu.HBM)
    vmem = pl.BlockSpec(memory_space=pltpu.VMEM)
    field = pltpu.VMEM((2, EX, EY, 128), F32)
    thin = pltpu.VMEM((EX, 8, 128), F32)
    inner = pltpu.VMEM((EX - 2, 8, 128), F32)
    dma = pltpu.SemaphoreType.DMA
    result = pl.pallas_call(
        kernel,
        out_shape=jax.ShapeDtypeStruct((xr, depth, yr), F32),
        in_specs=[hbm] * 7,
        out_specs=vmem,
        scratch_shapes=[
            pltpu.VMEM((xr, depth, yr), F32),
            pltpu.VMEM((depth, xr * yr), F32),
            pltpu.SMEM((2, 32), I32),
            pltpu.VMEM((2, 128), I32),
            pltpu.VMEM((32, 128), F32),
            pltpu.SMEM((32,), I32),
            field, field, field, field,
            pltpu.VMEM((EX, EY, 128), F32),
            pltpu.VMEM((6, EX, EY, 128), F32),
            pltpu.VMEM((6, CX, EY, 128), F32),
            pltpu.VMEM((128, 128), F32),
            pltpu.VMEM((XR, YR, 128), F32),
            pltpu.VMEM((128, EX * 128), BF16),
            pltpu.VMEM((128, CX * YR), BF16),
            thin,
            pltpu.VMEM((6, EX - 2, 8, 128), F32),
            inner, inner, thin, thin,
            pltpu.VMEM((2, 8, 128), F32),
            pltpu.VMEM((NZC - 1, 8, 128), F32),
            pltpu.VMEM((NGY - 1, 8, 128), F32),
            pltpu.VMEM((2, 128, 128), F32),
            pltpu.VMEM((2, NSRCG, 16, 128), F32),
            dma((5,)),
            dma((2, 2)), dma((2, 2)),
            *([dma] * 10),
        ],
        compiler_params=pltpu.CompilerParams(
            collective_id=0, has_side_effects=True, vmem_limit_bytes=63 * 1024 * 1024
        ),
    )(
        warm_potential, warm_adjoint, jnp.transpose(conductivity, (0, 2, 1)), electrodes.T, receivers.T,
        observed, source_order,
    )
    return jnp.transpose(result, (0, 2, 1))


def solution(mesh):
    in_specs = (
        P("src", "gx", "gy", None),
        P("src", "gx", "gy", None),
        P("gx", "gy", "src"),
        P(),
        P(),
        P(),
        P(),
    )
    out_specs = P("gx", "gy", "src")
    return jax.shard_map(body, mesh=mesh, in_specs=in_specs, out_specs=out_specs, check_vma=False)
```

```python
import functools

import jax
import jax.numpy as jnp
from jax import lax
from jax.experimental import pallas as pl
from jax.experimental.pallas import tpu as pltpu
from jax.sharding import PartitionSpec as P

MESH = pl.DeviceIdType.MESH
SWEEPS = 6
lowest = 0.05
highest = 2.0
centre = (highest + lowest) / 2.0
half_span = (highest - lowest) / 2.0
bound_ratio = centre / half_span
strength = 4.0

F32 = jnp.float32
I32 = jnp.int32
BF16 = jnp.bfloat16

NSRCG, NGX, NGY = 8, 16, 4
NZC = NGX // 2
NX, NY = 64, 128
XR, YR = 4, 32
CX = 2 * XR
HALO = 8
EX, EY = CX + 2 * HALO, YR + 2 * HALO


def chebyshev():
    out = []
    factor = 1.0 / bound_ratio
    for _ in range(SWEEPS):
        following = 1.0 / (2.0 * bound_ratio - factor)
        out.append((following * factor, 2.0 * following / half_span))
        factor = following
    return out


STEPS = chebyshev()
BLOCKS = {22: 11, 20: 10, 18: 9, 16: 8, 14: 7, 12: 12, 10: 10}


def split3(v):
    hi = v.astype(BF16)
    rest = v - hi.astype(F32)
    mid = rest.astype(BF16)
    lo = (rest - mid.astype(F32)).astype(BF16)
    return hi, mid, lo


def kernel(
    wp_ref, wa_ref, cond_hbm, elec_hbm, rec_hbm, obs_hbm, order_hbm,
    out_ref,
    cond_v, cond_ref, elec_ref, rec_v, obs_ref, order_ref,
    p0, p1, a0, a1, cext, coef, slope, gath, pan, pick,
    wp_v, flat_p, edge_p, thin_main, thin_edge,
    scond, scoef, sinv, srhs, y0, y1, vm, zbuf, gbuf, gt, rbuf,
    main_s, main_r, edge_s, edge_r,
    loc_sem, warm_s, warm_r, cond_s, cond_r, src_s, src_r, z_s, z_r, g_s, g_r, rs_s, rs_r,
):
    src = lax.axis_index("src")
    gx = lax.axis_index("gx")
    gy = lax.axis_index("gy")
    zc = gx // 2
    core = gx - 2 * zc

    def place(ds=0, dz=0, t=0, dg=0):
        z2 = lax.rem(zc + (dz % NZC), NZC)
        c2 = core if t == 0 else 1 - core
        return {
            "src": lax.rem(src + (ds % NSRCG), NSRCG),
            "gx": 2 * z2 + c2,
            "gy": lax.rem(gy + (dg % NGY), NGY),
        }

    halo = [
        (dz, t, dg)
        for dg in (0, 1, -1)
        for dz in (0, 1, -1)
        for t in (1, 0)
        if (dz, t, dg) != (0, 0, 0)
    ]

    partners = [place(dz=dz, t=t, dg=dg) for dz, t, dg in halo]
    partners += [place(ds=ds, t=t) for ds in range(1, NSRCG) for t in (0, 1)]
    partners += [place(dz=dz) for dz in range(2, NZC - 1)]
    partners += [place(dg=dg) for dg in range(2, NGY - 1)]
    barrier = pltpu.get_barrier_semaphore()
    for device in partners:
        pl.semaphore_signal(barrier, inc=1, device_id=device, device_id_type=MESH)

    own_x = pl.ds(HALO + XR * core, XR)
    def settle(ref, sem):
        pltpu.make_async_copy(ref, ref, sem).wait()

    owns = [
        pltpu.make_async_copy(
            ref.at[2 * core + slot], dest.at[slot, own_x, HALO : HALO + YR, :], warm_r.at[which, slot]
        )
        for which, (ref, dest) in enumerate(((wp_ref, p0), (wa_ref, a0)))
        for slot in range(2)
    ]
    small = [
        pltpu.make_async_copy(a, b, loc_sem.at[i])
        for i, (a, b) in enumerate(
            (
                (cond_hbm, cond_v), (rec_hbm, rec_v), (order_hbm, order_ref), (elec_hbm, elec_ref),
                (obs_hbm, obs_ref), (wp_ref, wp_v),
            )
        )
    ]
    for copy in small:
        copy.start()
    for copy in owns:
        copy.start()
    for copy in small:
        copy.wait()

    own_rows = pl.ds(pl.multiple_of(16 * src, 16), 16)
    piece = jnp.concatenate([cond_v[x] for x in range(XR)], axis=1)
    cond_ref[...] = piece
    pltpu.make_async_copy(cond_ref, gath.at[own_rows, :], src_r).start()

    for x in range(XR):
        flat_p[x] = jnp.transpose(wp_v[:, x].reshape(128, 128))[0:8]
    for side, ys in enumerate((slice(YR - HALO, YR), slice(0, HALO))):
        edge_p[side] = jnp.transpose(wp_v[:, :, ys, :].reshape(128, 128))[0:8]
    pltpu.make_async_copy(flat_p, thin_main.at[own_x], main_r).start()

    pl.semaphore_wait(barrier, len(partners))

    gathers = [
        pltpu.make_async_remote_copy(
            cond_ref, gath.at[own_rows, :], src_s, src_r,
            device_id=place(ds=ds), device_id_type=MESH,
        )
        for ds in range(1, NSRCG)
    ]
    for copy in gathers:
        copy.start()

    def y_spans(dg):
        if dg == 0:
            return slice(0, YR), slice(HALO, HALO + YR)
        if dg == 1:
            return slice(YR - HALO, YR), slice(0, HALO)
        return slice(0, HALO), slice(HALO + YR, EY)

    def warm_copies(which, ref, dest, slot):
        copies = []
        for dz, t, dg in halo:
            ys, yd = y_spans(dg)
            c2 = core if t == 0 else 1 - core
            copies.append(
                pltpu.make_async_remote_copy(
                    ref.at[2 * c2 + slot, :, ys, :],
                    dest.at[slot, pl.ds(HALO * (1 - dz) + XR * core, XR), yd, :],
                    warm_s.at[which, slot], warm_r.at[which, slot],
                    device_id=place(dz=dz, t=t, dg=dg), device_id_type=MESH,
                )
            )
        return copies

    copies_p = [warm_copies(0, wp_ref, p0, slot) for slot in range(2)]
    copies_a = [warm_copies(1, wa_ref, a0, slot) for slot in range(2)]
    for dz, t, dg in halo:
        if dg == 0:
            a, b = flat_p, thin_main.at[pl.ds(HALO * (1 - dz) + XR * core, XR)]
            sems = main_s, main_r
        else:
            side = 0 if dg == 1 else 1
            a, b = edge_p.at[side], thin_edge.at[side, 2 * (1 - dz) + core]
            sems = edge_s, edge_r
        pltpu.make_async_remote_copy(
            a, b, *sems, device_id=place(dz=dz, t=t, dg=dg), device_id_type=MESH
        ).start()
    for copy in copies_p[0]:
        copy.start()

    cells = jnp.concatenate([rec_v[...].astype(F32), jnp.zeros((126, 128), F32)], axis=0)
    cells = jnp.transpose(cells).astype(I32)
    rx0 = cells[:, 0:1] >> 7
    ry0 = cells[:, 0:1] & (NY - 1)
    rx1 = cells[:, 1:2] >> 7
    ry1 = cells[:, 1:2] & (NY - 1)

    lanes = lax.broadcasted_iota(I32, (128, 128), 1)
    ylane = lanes & 63
    ycell = (YR * gy - HALO + ylane) & (NY - 1)
    ok0 = (ry0 == ycell) & (ylane < EY)
    ok1 = (ry1 == ycell) & (ylane < EY)
    col0 = jnp.where(ok0, rx0, -1)
    col1 = jnp.where(ok1, rx1, -1)
    for r in range(EX):
        xrow = (CX * zc - HALO + r) & (NX - 1)
        pick[:, r * 128 : (r + 1) * 128] = (
            jnp.where(col0 == xrow, 1.0, 0.0) - jnp.where(col1 == xrow, 1.0, 0.0)
        ).astype(BF16)

    settle(gath, src_r)
    pan[...] = jnp.transpose(gath[...]).reshape(XR, YR, 128)
    pltpu.make_async_copy(pan, cext.at[own_x, HALO : HALO + YR, :], cond_r).start()
    copies_c = []
    for dz, t, dg in halo:
        ys, yd = y_spans(dg)
        copies_c.append(
            pltpu.make_async_remote_copy(
                pan.at[:, ys, :],
                cext.at[pl.ds(HALO * (1 - dz) + XR * core, XR), yd, :],
                cond_s, cond_r,
                device_id=place(dz=dz, t=t, dg=dg), device_id_type=MESH,
            )
        )
    for copy in copies_c:
        copy.start()
    for copy in copies_p[1]:
        copy.start()
    settle(cext, cond_r)

    yy = (YR * gy - HALO + lax.broadcasted_iota(I32, (EY, 128), 0)) & (NY - 1)
    zz = lax.broadcasted_iota(I32, (EY, 128), 1)
    in_ym = yy != 0
    in_yp = yy != NY - 1
    in_zm = zz != 0
    in_zp = zz != 127

    def x_inside(r):
        row = (CX * zc - HALO + r) & (NX - 1)
        return jnp.where(row == 0, 0.0, 1.0).astype(F32), jnp.where(row == NX - 1, 0.0, 1.0).astype(F32)

    def harmonic(s, n):
        return 2.0 * s * n / (s + n)

    for first, count in ((0, 16), (16, 8)):
        gathered = jnp.ones((EY, 128), F32)
        for i in range(count):
            rolled = pltpu.roll(cext[first + i], 8 * i, 1) if i else cext[first]
            gathered = jnp.where((zz >= 8 * i) & (zz < 8 * i + 8), rolled, gathered)
        ones = jnp.ones((64 - EY, 128), F32)
        turned = jnp.transpose(jnp.concatenate([gathered, ones, gathered, ones], axis=0))
        scond[first : first + count] = turned[: 8 * count].reshape(count, 8, 128)

    shape = (EX - 2, 8, 128)
    lane3 = lax.broadcasted_iota(I32, shape, 2)
    sub3 = lax.broadcasted_iota(I32, shape, 1)
    row3 = (lax.broadcasted_iota(I32, shape, 0) + (CX * zc - HALO + 1)) & (NX - 1)
    y3 = (YR * gy - HALO + (lane3 & 63)) & (NY - 1)
    s = scond[1 : EX - 1]
    hs = [
        (harmonic(s, scond[0 : EX - 2]), row3 != 0, True),
        (harmonic(s, scond[2:EX]), row3 != NX - 1, True),
        (harmonic(s, pltpu.roll(s, 1, 2)), y3 != 0, True),
        (harmonic(s, pltpu.roll(s, 127, 2)), y3 != NY - 1, True),
        (harmonic(s, pltpu.roll(s, 1, 1)), sub3 != 0, False),
        (harmonic(s, pltpu.roll(s, 7, 1)), sub3 != 7, False),
    ]
    diag = jnp.zeros(shape, F32)
    for h, inside, outer in hs:
        diag = diag + jnp.where(inside, h, s if outer else 0.0)
    inv = 1.0 / diag
    sinv[...] = inv
    for i, (h, inside, outer) in enumerate(hs):
        scoef[i] = jnp.where(inside, h, 0.0) * inv

    def thin_apply(x):
        u = x[1 : EX - 1]
        total = scoef[0] * x[0 : EX - 2] + scoef[1] * x[2:EX]
        total = total + scoef[2] * pltpu.roll(u, 1, 2) + scoef[3] * pltpu.roll(u, 127, 2)
        total = total + scoef[4] * pltpu.roll(u, 1, 1) + scoef[5] * pltpu.roll(u, 7, 1)
        return u, sinv[...] * srhs[...] + total

    def thin_solve(started):
        zero = jnp.zeros((1, 8, 128), F32)
        for ref in (y1,) if started else (y0, y1):
            ref[0:1] = zero
            ref[EX - 1 : EX] = zero
        if started:
            u, total = thin_apply(y0)
            y1[1 : EX - 1] = (1.0 - 1.0 / centre) * u + (1.0 / centre) * total
        else:
            y0[1 : EX - 1] = jnp.zeros(shape, F32)
            y1[1 : EX - 1] = sinv[...] * srhs[...] * (1.0 / centre)
        older, newer = y0, y1
        for a, b in STEPS:
            u, total = thin_apply(newer)
            older[1 : EX - 1] = (1.0 + a - b) * u - a * older[1 : EX - 1] + b * total
            older, newer = newer, older
        return newer

    def add_thin(thin, dest):
        first = HALO - 1
        turned = jnp.transpose(thin[first : first + 16].reshape(128, 128))
        shallow = lanes < 8
        for i in range(CX + 2):
            part = jnp.where(shallow, pltpu.roll(turned, (128 - 8 * i) % 128, 1) if i else turned, 0.0)
            for slot in range(2):
                dest[slot, first + i] = dest[slot, first + i] + part[64 * slot : 64 * slot + EY]

    first_slot = 4 * src + 2 * core
    idents = [order_ref[first_slot + j] for j in range(2)]
    rhs = jnp.zeros(shape, F32)
    for e, sign in ((0, strength), (1, -strength)):
        cells = [elec_ref[e, k] for k in idents]
        ex = jnp.where(lane3 < 64, cells[0] >> 7, cells[1] >> 7)
        ey = jnp.where(lane3 < 64, cells[0] & (NY - 1), cells[1] & (NY - 1))
        hit = (ex == row3) & (ey == y3) & (sub3 == 0) & ((lane3 & 63) < EY)
        rhs = rhs + jnp.where(hit, sign, 0.0)
    srhs[...] = rhs

    settle(thin_main, main_r)
    settle(thin_edge, edge_r)
    lane1 = lax.broadcasted_iota(I32, (8, 128), 1)
    ylane1 = lane1 & 63

    def mine(block):
        return jnp.where(core == 0, block, pltpu.roll(block, 64, 1))

    for r in range(EX):
        row = mine(thin_main[r])
        low = mine(thin_edge[0, r // XR])
        high = mine(thin_edge[1, r // XR])
        start = jnp.zeros((8, 128), F32)
        for j in range(2):
            own_lane = (lane1 >> 6) == j
            for block, first, at, width in (
                (row, 32 * j, HALO, YR),
                (low, 32 * j + 8 * (r % XR), 0, HALO),
                (high, 32 * j + 8 * (r % XR), HALO + YR, HALO),
            ):
                shift = (64 * j + at - first) % 128
                moved = pltpu.roll(block, shift, 1) if shift else block
                start = jnp.where(own_lane & (ylane1 >= at) & (ylane1 < at + width), moved, start)
        y0[r] = start
    seen_p = thin_solve(True)
    sub1 = lax.broadcasted_iota(I32, (8, 128), 0)
    keep = (sub1 == (lane1 >> 6)) & (ylane1 >= HALO) & (ylane1 < HALO + YR)
    top = jnp.concatenate(
        [jnp.where(keep, jnp.broadcast_to(seen_p[HALO + i][0:1], (8, 128)), 0.0) for i in range(CX)], axis=1
    )
    hi, mid, lo = split3(top)
    stacked = jnp.concatenate(
        [hi.astype(F32), mid.astype(F32), lo.astype(F32), jnp.zeros((8, CX * 128), F32)], axis=0
    ).astype(BF16)
    got = lax.dot_general(
        stacked, pick[:, HALO * 128 : (HALO + CX) * 128], (((1,), (1,)), ((), ())), preferred_element_type=F32
    )
    vm[0] = got[0:8] + got[8:16] + got[16:24]
    copies_z = [
        pltpu.make_async_remote_copy(
            vm.at[0], zbuf.at[dz - 1], z_s, z_r,
            device_id=place(dz=dz), device_id_type=MESH,
        )
        for dz in range(1, NZC)
    ]
    for copy in copies_z:
        copy.start()
    thin_p = thin_solve(False)
    for copy in copies_a[0]:
        copy.start()


    def coef_row(r, carry):
        s = cext[r]
        fm, fp = x_inside(r)
        hxm = harmonic(s, cext[r - 1]) * fm
        hxp = harmonic(s, cext[r + 1]) * fp
        hym = jnp.where(in_ym, harmonic(s, pltpu.roll(s, 1, 0)), 0.0)
        hyp = jnp.where(in_yp, harmonic(s, pltpu.roll(s, EY - 1, 0)), 0.0)
        hzm = jnp.where(in_zm, harmonic(s, pltpu.roll(s, 1, 1)), 0.0)
        hzp = jnp.where(in_zp, harmonic(s, pltpu.roll(s, 127, 1)), 0.0)
        diag = hxm + hxp + hym + hyp + hzm + hzp
        diag = diag + s * ((1.0 - fm) + (1.0 - fp))
        diag = diag + jnp.where(in_ym, 0.0, s) + jnp.where(in_yp, 0.0, s) + jnp.where(in_zp, 0.0, s)
        inv = 1.0 / diag
        for i, h in enumerate((hxm, hxp, hym, hyp, hzm, hzp)):
            coef[i, r] = h * inv
        return carry

    lax.fori_loop(1, EX - 1, coef_row, 0, unroll=2)

    def slope_of(s, n):
        total = s + n
        return 2.0 * n * n / (total * total)

    def slope_row(r, carry):
        s = cext[r]
        fm, fp = x_inside(r)
        q = r - HALO
        slope[0, q] = slope_of(s, cext[r - 1]) * fm + (1.0 - fm)
        slope[1, q] = slope_of(s, cext[r + 1]) * fp + (1.0 - fp)
        slope[2, q] = jnp.where(in_ym, slope_of(s, pltpu.roll(s, 1, 0)), 1.0)
        slope[3, q] = jnp.where(in_yp, slope_of(s, pltpu.roll(s, EY - 1, 0)), 1.0)
        slope[4, q] = jnp.where(in_zm, slope_of(s, pltpu.roll(s, 1, 1)), 0.0)
        slope[5, q] = jnp.where(in_zp, slope_of(s, pltpu.roll(s, 127, 1)), 1.0)
        return carry

    def app(slot, x, prev, dest, wc, wu, wp, e):
        rows = CX + 2 * e
        block = BLOCKS[rows]

        def step(q, carry):
            fresh = []
            for i in range(block):
                r = HALO - e + q * block + i
                u = x[slot, r]
                total = coef[0, r] * x[slot, r - 1] + coef[1, r] * x[slot, r + 1]
                total = total + coef[2, r] * pltpu.roll(u, 1, 0) + coef[3, r] * pltpu.roll(u, EY - 1, 0)
                total = total + coef[4, r] * pltpu.roll(u, 1, 1) + coef[5, r] * pltpu.roll(u, 127, 1)
                value = wu * u + wc * total
                if prev is not None:
                    value = value - wp * prev[slot, r]
                fresh.append((r, value))
            for r, value in fresh:
                dest[slot, r] = value
            return carry

        lax.fori_loop(0, rows // block, step, 0)

    def full_solve(which, slot, x0, x1):
        settle(x0.at[slot], warm_r.at[which, slot])
        app(slot, x0, None, x1, 1.0 / centre, 1.0 - 1.0 / centre, 0.0, HALO - 1)
        for k, (a, b) in enumerate(STEPS):
            older, newer = (x1, x0) if k % 2 else (x0, x1)
            app(slot, newer, older, older, b, 1.0 + a - b, a, HALO - 2 - k)

    pot, adj = p1, a1
    full_solve(0, 0, p0, p1)

    settle(zbuf, z_r)
    total = vm[0]
    for i in range(NZC - 1):
        total = total + zbuf[i]
    vm[1] = total
    copies_g = [
        pltpu.make_async_remote_copy(
            vm.at[1], gbuf.at[dg - 1], g_s, g_r,
            device_id=place(dg=dg), device_id_type=MESH,
        )
        for dg in range(1, NGY)
    ]
    for copy in copies_g:
        copy.start()
    for copy in copies_a[1]:
        copy.start()
    full_solve(0, 1, p0, p1)
    add_thin(thin_p, pot)

    lax.fori_loop(HALO, HALO + CX, slope_row, 0, unroll=2)
    full_solve(1, 0, a0, a1)


    full_solve(1, 1, a0, a1)
    settle(gbuf, g_r)
    total = vm[1]
    for i in range(NGY - 1):
        total = total + gbuf[i]
    sub8 = lax.broadcasted_iota(I32, (8, 128), 0)
    lane8 = lax.broadcasted_iota(I32, (8, 128), 1)
    seen = jnp.where(sub8 == 0, obs_ref[pl.ds(idents[0], 1), :], obs_ref[pl.ds(idents[1], 1), :])
    misfit = jnp.where(sub8 < 2, total - seen, 0.0)
    hi, mid, lo = split3(misfit)
    stacked = jnp.concatenate(
        [hi.astype(F32), mid.astype(F32), lo.astype(F32), jnp.zeros((8, 128), F32)], axis=0
    ).astype(BF16)
    back = jnp.dot(stacked, pick[...], preferred_element_type=F32)
    for r in range(1, EX - 1):
        cut = back[:, r * 128 : (r + 1) * 128]
        both = cut[0:8] + cut[8:16] + cut[16:24]
        line = jnp.where(lane8[0:1] < 64, both[0:1], both[1:2])
        srhs[r - 1] = jnp.where(sub8 == 0, line, 0.0)
    thin_a = thin_solve(False)
    add_thin(thin_a, adj)

    def grad_row(r, carry):
        q = r - HALO
        fm, fp = x_inside(r)
        sums = [jnp.zeros((EY, 128), F32) for _ in range(6)]
        for slot in range(2):
            p = pot[slot, r]
            a = adj[slot, r]
            near = [
                (pot[slot, r - 1] * fm, adj[slot, r - 1] * fm),
                (pot[slot, r + 1] * fp, adj[slot, r + 1] * fp),
            ]
            for inside, shift, axis in ((in_ym, 1, 0), (in_yp, EY - 1, 0), (in_zm, 1, 1), (in_zp, 127, 1)):
                near.append(
                    (
                        jnp.where(inside, pltpu.roll(p, shift, axis), 0.0),
                        jnp.where(inside, pltpu.roll(a, shift, axis), 0.0),
                    )
                )
            sums = [old + (p - pn) * (a - an) for old, (pn, an) in zip(sums, near)]
        out = slope[0, q] * sums[0]
        for i in range(1, 6):
            out = out + slope[i, q] * sums[i]
        pan8[q] = out[HALO : HALO + YR]
        return carry

    pan8 = slope.at[0, :, 0:YR, :]

    lax.fori_loop(HALO, HALO + CX, grad_row, 0, unroll=2)
    for c in range(2):
        gt[c] = jnp.transpose(slope[0, XR * c : XR * c + XR, 0:YR, :].reshape(128, 128))

    def rs_copy(ds, t):
        c2 = core if t == 0 else 1 - core
        s2 = lax.rem(src + ds, NSRCG)
        return pltpu.make_async_remote_copy(
            gt.at[c2, pl.ds(pl.multiple_of(16 * s2, 16), 16), :],
            rbuf.at[t, ds],
            rs_s, rs_r,
            device_id=place(ds=ds, t=t), device_id_type=MESH,
        )

    copies_rs = [rs_copy(ds, t) for ds in range(NSRCG) for t in (0, 1) if ds or t]
    for copy in copies_rs:
        copy.start()
    pltpu.make_async_copy(gt.at[core, own_rows, :], rbuf.at[0, 0], rs_r).start()
    settle(rbuf, rs_r)
    total = rbuf[0, 0] + rbuf[1, 0]
    for ds in range(1, NSRCG):
        total = total + (rbuf[0, ds] + rbuf[1, ds])
    total = -total
    for x in range(XR):
        out_ref[x] = (pltpu.roll(total, 128 - YR * x, 1) if x else total)[:, :YR]

    sent = p0.at[:, 0:16, 0:YR, :]
    for which in range(2):
        for slot in range(2):
            settle(sent, warm_s.at[which, slot])
    settle(sent, cond_s)
    settle(gath.at[0 : 16 * (NSRCG - 1), :], src_s)
    settle(thin_main.at[0 : 5 * XR], main_s)
    settle(thin_edge, edge_s)
    settle(zbuf, z_s)
    settle(gbuf, g_s)
    settle(gt.at[:, 0 : 8 * (2 * NSRCG - 1), :], rs_s)


def body(warm_potential, warm_adjoint, conductivity, electrodes, receivers, observed, source_order):
    xr, yr, depth = conductivity.shape
    hbm = pl.BlockSpec(memory_space=pltpu.HBM)
    vmem = pl.BlockSpec(memory_space=pltpu.VMEM)
    field = pltpu.VMEM((2, EX, EY, 128), F32)
    thin = pltpu.VMEM((EX, 8, 128), F32)
    inner = pltpu.VMEM((EX - 2, 8, 128), F32)
    dma = pltpu.SemaphoreType.DMA
    result = pl.pallas_call(
        kernel,
        out_shape=jax.ShapeDtypeStruct((xr, depth, yr), F32),
        in_specs=[hbm] * 7,
        out_specs=vmem,
        scratch_shapes=[
            pltpu.VMEM((xr, depth, yr), F32),
            pltpu.VMEM((depth, xr * yr), F32),
            pltpu.SMEM((2, 32), I32),
            pltpu.VMEM((2, 128), I32),
            pltpu.VMEM((32, 128), F32),
            pltpu.SMEM((32,), I32),
            field, field, field, field,
            pltpu.VMEM((EX, EY, 128), F32),
            pltpu.VMEM((6, EX, EY, 128), F32),
            pltpu.VMEM((6, CX, EY, 128), F32),
            pltpu.VMEM((128, 128), F32),
            pltpu.VMEM((XR, YR, 128), F32),
            pltpu.VMEM((128, EX * 128), BF16),
            pltpu.VMEM((4, XR, YR, 128), F32),
            pltpu.VMEM((XR, 8, 128), F32),
            pltpu.VMEM((2, 8, 128), F32),
            thin,
            pltpu.VMEM((2, 6, 8, 128), F32),
            thin,
            pltpu.VMEM((6, EX - 2, 8, 128), F32),
            inner, inner, thin, thin,
            pltpu.VMEM((2, 8, 128), F32),
            pltpu.VMEM((NZC - 1, 8, 128), F32),
            pltpu.VMEM((NGY - 1, 8, 128), F32),
            pltpu.VMEM((2, 128, 128), F32),
            pltpu.VMEM((2, NSRCG, 16, 128), F32),
            dma, dma, dma, dma,
            dma((6,)),
            dma((2, 2)), dma((2, 2)),
            *([dma] * 10),
        ],
        compiler_params=pltpu.CompilerParams(
            collective_id=0, has_side_effects=True, vmem_limit_bytes=63 * 1024 * 1024
        ),
    )(
        warm_potential, warm_adjoint, jnp.transpose(conductivity, (0, 2, 1)), electrodes.T, receivers.T,
        observed, source_order,
    )
    return jnp.transpose(result, (0, 2, 1))


def solution(mesh):
    in_specs = (
        P("src", "gx", "gy", None),
        P("src", "gx", "gy", None),
        P("gx", "gy", "src"),
        P(),
        P(),
        P(),
        P(),
    )
    out_specs = P("gx", "gy", "src")
    return jax.shard_map(body, mesh=mesh, in_specs=in_specs, out_specs=out_specs, check_vma=False)
```

```python
import functools

import jax
import jax.numpy as jnp
from jax import lax
from jax.experimental import pallas as pl
from jax.experimental.pallas import tpu as pltpu
from jax.sharding import PartitionSpec as P

MESH = pl.DeviceIdType.MESH
SWEEPS = 6
lowest = 0.05
highest = 2.0
centre = (highest + lowest) / 2.0
half_span = (highest - lowest) / 2.0
bound_ratio = centre / half_span
strength = 4.0

F32 = jnp.float32
I32 = jnp.int32
BF16 = jnp.bfloat16

NSRCG, NGX, NGY = 8, 16, 4
NZC = NGX // 2
NX, NY = 64, 128
XR, YR = 4, 32
CX = 2 * XR
HALO = 8
EX, EY = CX + 2 * HALO, YR + 2 * HALO


def chebyshev():
    out = []
    factor = 1.0 / bound_ratio
    for _ in range(SWEEPS):
        following = 1.0 / (2.0 * bound_ratio - factor)
        out.append((following * factor, 2.0 * following / half_span))
        factor = following
    return out


STEPS = chebyshev()
BLOCKS = {22: 11, 20: 10, 18: 9, 16: 8, 14: 7, 12: 12, 10: 10}


def split3(v):
    hi = v.astype(BF16)
    rest = v - hi.astype(F32)
    mid = rest.astype(BF16)
    lo = (rest - mid.astype(F32)).astype(BF16)
    return hi, mid, lo


def kernel(
    wp_ref, wa_ref, cond_hbm, elec_hbm, rec_hbm, obs_hbm, order_hbm,
    out_ref,
    cond_v, cond_ref, elec_ref, rec_v, obs_ref, order_ref,
    p0, p1, a0, a1, cext, coef, slope, gath, pan, pick,
    wp_v, flat_p, edge_p, thin_main, thin_edge,
    scond, scoef, sinv, srhs, y0, y1, vm, zbuf, gbuf, gt, rbuf,
    main_s, main_r, edge_s, edge_r,
    loc_sem, warm_s, warm_r, cond_s, cond_r, src_s, src_r, z_s, z_r, g_s, g_r, rs_s, rs_r,
):
    src = lax.axis_index("src")
    gx = lax.axis_index("gx")
    gy = lax.axis_index("gy")
    zc = gx // 2
    core = gx - 2 * zc

    def place(ds=0, dz=0, t=0, dg=0):
        z2 = lax.rem(zc + (dz % NZC), NZC)
        c2 = core if t == 0 else 1 - core
        return {
            "src": lax.rem(src + (ds % NSRCG), NSRCG),
            "gx": 2 * z2 + c2,
            "gy": lax.rem(gy + (dg % NGY), NGY),
        }

    halo = [
        (dz, t, dg)
        for dg in (0, 1, -1)
        for dz in (0, 1, -1)
        for t in (1, 0)
        if (dz, t, dg) != (0, 0, 0)
    ]

    partners = [place(dz=dz, t=t, dg=dg) for dz, t, dg in halo]
    partners += [place(ds=ds, t=t) for ds in range(1, NSRCG) for t in (0, 1)]
    partners += [place(dz=dz) for dz in range(2, NZC - 1)]
    partners += [place(dg=dg) for dg in range(2, NGY - 1)]
    barrier = pltpu.get_barrier_semaphore()
    for device in partners:
        pl.semaphore_signal(barrier, inc=1, device_id=device, device_id_type=MESH)

    own_x = pl.ds(HALO + XR * core, XR)
    def settle(ref, sem):
        pltpu.make_async_copy(ref, ref, sem).wait()

    owns = [
        pltpu.make_async_copy(
            ref.at[2 * core + slot], dest.at[slot, own_x, HALO : HALO + YR, :], warm_r.at[which, slot]
        )
        for which, (ref, dest) in enumerate(((wp_ref, p0), (wa_ref, a0)))
        for slot in range(2)
    ]
    small = [
        pltpu.make_async_copy(a, b, loc_sem.at[i])
        for i, (a, b) in enumerate(
            (
                (cond_hbm, cond_v), (rec_hbm, rec_v), (order_hbm, order_ref), (elec_hbm, elec_ref),
                (obs_hbm, obs_ref), (wp_ref, wp_v),
            )
        )
    ]
    for copy in small:
        copy.start()
    for copy in owns:
        copy.start()
    for copy in small:
        copy.wait()

    own_rows = pl.ds(pl.multiple_of(16 * src, 16), 16)
    piece = jnp.concatenate([cond_v[x] for x in range(XR)], axis=1)
    cond_ref[...] = piece
    pltpu.make_async_copy(cond_ref, gath.at[own_rows, :], src_r).start()

    for x in range(XR):
        flat_p[x] = jnp.transpose(wp_v[:, x].reshape(128, 128))[0:8]
    for side, ys in enumerate((slice(YR - HALO, YR), slice(0, HALO))):
        edge_p[side] = jnp.transpose(wp_v[:, :, ys, :].reshape(128, 128))[0:8]
    pltpu.make_async_copy(flat_p, thin_main.at[own_x], main_r).start()

    pl.semaphore_wait(barrier, len(partners))

    gathers = [
        pltpu.make_async_remote_copy(
            cond_ref, gath.at[own_rows, :], src_s, src_r,
            device_id=place(ds=ds), device_id_type=MESH,
        )
        for ds in range(1, NSRCG)
    ]
    for copy in gathers:
        copy.start()

    def y_spans(dg):
        if dg == 0:
            return slice(0, YR), slice(HALO, HALO + YR)
        if dg == 1:
            return slice(YR - HALO, YR), slice(0, HALO)
        return slice(0, HALO), slice(HALO + YR, EY)

    def warm_copies(which, ref, dest, slot):
        copies = []
        for dz, t, dg in halo:
            ys, yd = y_spans(dg)
            c2 = core if t == 0 else 1 - core
            copies.append(
                pltpu.make_async_remote_copy(
                    ref.at[2 * c2 + slot, :, ys, :],
                    dest.at[slot, pl.ds(HALO * (1 - dz) + XR * core, XR), yd, :],
                    warm_s.at[which, slot], warm_r.at[which, slot],
                    device_id=place(dz=dz, t=t, dg=dg), device_id_type=MESH,
                )
            )
        return copies

    copies_p = [warm_copies(0, wp_ref, p0, slot) for slot in range(2)]
    copies_a = [warm_copies(1, wa_ref, a0, slot) for slot in range(2)]
    for dz, t, dg in halo:
        if dg == 0:
            a, b = flat_p, thin_main.at[pl.ds(HALO * (1 - dz) + XR * core, XR)]
            sems = main_s, main_r
        else:
            side = 0 if dg == 1 else 1
            a, b = edge_p.at[side], thin_edge.at[side, 2 * (1 - dz) + core]
            sems = edge_s, edge_r
        pltpu.make_async_remote_copy(
            a, b, *sems, device_id=place(dz=dz, t=t, dg=dg), device_id_type=MESH
        ).start()
    for copy in copies_p[0]:
        copy.start()

    cells = jnp.concatenate([rec_v[...].astype(F32), jnp.zeros((126, 128), F32)], axis=0)
    cells = jnp.transpose(cells).astype(I32)
    rx0 = cells[:, 0:1] >> 7
    ry0 = cells[:, 0:1] & (NY - 1)
    rx1 = cells[:, 1:2] >> 7
    ry1 = cells[:, 1:2] & (NY - 1)

    lanes = lax.broadcasted_iota(I32, (128, 128), 1)
    ylane = lanes & 63
    ycell = (YR * gy - HALO + ylane) & (NY - 1)
    ok0 = (ry0 == ycell) & (ylane < EY)
    ok1 = (ry1 == ycell) & (ylane < EY)
    col0 = jnp.where(ok0, rx0, -1)
    col1 = jnp.where(ok1, rx1, -1)
    for r in range(EX):
        xrow = (CX * zc - HALO + r) & (NX - 1)
        pick[:, r * 128 : (r + 1) * 128] = (
            jnp.where(col0 == xrow, 1.0, 0.0) - jnp.where(col1 == xrow, 1.0, 0.0)
        ).astype(BF16)

    settle(gath, src_r)
    pan[...] = jnp.transpose(gath[...]).reshape(XR, YR, 128)
    pltpu.make_async_copy(pan, cext.at[own_x, HALO : HALO + YR, :], cond_r).start()
    copies_c = []
    for dz, t, dg in halo:
        ys, yd = y_spans(dg)
        copies_c.append(
            pltpu.make_async_remote_copy(
                pan.at[:, ys, :],
                cext.at[pl.ds(HALO * (1 - dz) + XR * core, XR), yd, :],
                cond_s, cond_r,
                device_id=place(dz=dz, t=t, dg=dg), device_id_type=MESH,
            )
        )
    for copy in copies_c:
        copy.start()
    for copy in copies_p[1]:
        copy.start()
    settle(cext, cond_r)

    yy = (YR * gy - HALO + lax.broadcasted_iota(I32, (EY, 128), 0)) & (NY - 1)
    zz = lax.broadcasted_iota(I32, (EY, 128), 1)
    in_ym = yy != 0
    in_yp = yy != NY - 1
    in_zm = zz != 0
    in_zp = zz != 127

    def x_inside(r):
        row = (CX * zc - HALO + r) & (NX - 1)
        return jnp.where(row == 0, 0.0, 1.0).astype(F32), jnp.where(row == NX - 1, 0.0, 1.0).astype(F32)

    def harmonic(s, n):
        return 2.0 * s * n / (s + n)

    for first, count in ((0, 16), (16, 8)):
        gathered = jnp.ones((EY, 128), F32)
        for i in range(count):
            rolled = pltpu.roll(cext[first + i], 8 * i, 1) if i else cext[first]
            gathered = jnp.where((zz >= 8 * i) & (zz < 8 * i + 8), rolled, gathered)
        ones = jnp.ones((64 - EY, 128), F32)
        turned = jnp.transpose(jnp.concatenate([gathered, ones, gathered, ones], axis=0))
        scond[first : first + count] = turned[: 8 * count].reshape(count, 8, 128)

    shape = (EX - 2, 8, 128)
    lane3 = lax.broadcasted_iota(I32, shape, 2)
    sub3 = lax.broadcasted_iota(I32, shape, 1)
    row3 = (lax.broadcasted_iota(I32, shape, 0) + (CX * zc - HALO + 1)) & (NX - 1)
    y3 = (YR * gy - HALO + (lane3 & 63)) & (NY - 1)
    s = scond[1 : EX - 1]
    hs = [
        (harmonic(s, scond[0 : EX - 2]), row3 != 0, True),
        (harmonic(s, scond[2:EX]), row3 != NX - 1, True),
        (harmonic(s, pltpu.roll(s, 1, 2)), y3 != 0, True),
        (harmonic(s, pltpu.roll(s, 127, 2)), y3 != NY - 1, True),
        (harmonic(s, pltpu.roll(s, 1, 1)), sub3 != 0, False),
        (harmonic(s, pltpu.roll(s, 7, 1)), sub3 != 7, False),
    ]
    diag = jnp.zeros(shape, F32)
    for h, inside, outer in hs:
        diag = diag + jnp.where(inside, h, s if outer else 0.0)
    inv = 1.0 / diag
    sinv[...] = inv
    for i, (h, inside, outer) in enumerate(hs):
        scoef[i] = jnp.where(inside, h, 0.0) * inv

    def thin_apply(x):
        u = x[1 : EX - 1]
        total = scoef[0] * x[0 : EX - 2] + scoef[1] * x[2:EX]
        total = total + scoef[2] * pltpu.roll(u, 1, 2) + scoef[3] * pltpu.roll(u, 127, 2)
        total = total + scoef[4] * pltpu.roll(u, 1, 1) + scoef[5] * pltpu.roll(u, 7, 1)
        return u, sinv[...] * srhs[...] + total

    def thin_solve(started):
        zero = jnp.zeros((1, 8, 128), F32)
        for ref in (y1,) if started else (y0, y1):
            ref[0:1] = zero
            ref[EX - 1 : EX] = zero
        if started:
            u, total = thin_apply(y0)
            y1[1 : EX - 1] = (1.0 - 1.0 / centre) * u + (1.0 / centre) * total
        else:
            y0[1 : EX - 1] = jnp.zeros(shape, F32)
            y1[1 : EX - 1] = sinv[...] * srhs[...] * (1.0 / centre)
        older, newer = y0, y1
        for a, b in STEPS:
            u, total = thin_apply(newer)
            older[1 : EX - 1] = (1.0 + a - b) * u - a * older[1 : EX - 1] + b * total
            older, newer = newer, older
        return newer

    def add_thin(thin, dest):
        first = HALO - 1
        turned = jnp.transpose(thin[first : first + 16].reshape(128, 128))
        shallow = lanes < 8
        for i in range(CX + 2):
            part = jnp.where(shallow, pltpu.roll(turned, (128 - 8 * i) % 128, 1) if i else turned, 0.0)
            for slot in range(2):
                dest[slot, first + i] = dest[slot, first + i] + part[64 * slot : 64 * slot + EY]

    first_slot = 4 * src + 2 * core
    idents = [order_ref[first_slot + j] for j in range(2)]
    rhs = jnp.zeros(shape, F32)
    for e, sign in ((0, strength), (1, -strength)):
        cells = [elec_ref[e, k] for k in idents]
        ex = jnp.where(lane3 < 64, cells[0] >> 7, cells[1] >> 7)
        ey = jnp.where(lane3 < 64, cells[0] & (NY - 1), cells[1] & (NY - 1))
        hit = (ex == row3) & (ey == y3) & (sub3 == 0) & ((lane3 & 63) < EY)
        rhs = rhs + jnp.where(hit, sign, 0.0)
    srhs[...] = rhs

    settle(thin_main, main_r)
    settle(thin_edge, edge_r)
    lane1 = lax.broadcasted_iota(I32, (8, 128), 1)
    ylane1 = lane1 & 63

    def mine(block):
        return jnp.where(core == 0, block, pltpu.roll(block, 64, 1))

    for r in range(EX):
        row = mine(thin_main[r])
        low = mine(thin_edge[0, r // XR])
        high = mine(thin_edge[1, r // XR])
        start = jnp.zeros((8, 128), F32)
        for j in range(2):
            own_lane = (lane1 >> 6) == j
            for block, first, at, width in (
                (row, 32 * j, HALO, YR),
                (low, 32 * j + 8 * (r % XR), 0, HALO),
                (high, 32 * j + 8 * (r % XR), HALO + YR, HALO),
            ):
                shift = (64 * j + at - first) % 128
                moved = pltpu.roll(block, shift, 1) if shift else block
                start = jnp.where(own_lane & (ylane1 >= at) & (ylane1 < at + width), moved, start)
        y0[r] = start
    seen_p = thin_solve(True)
    sub1 = lax.broadcasted_iota(I32, (8, 128), 0)
    keep = (sub1 == (lane1 >> 6)) & (ylane1 >= HALO) & (ylane1 < HALO + YR)
    top = jnp.concatenate(
        [jnp.where(keep, jnp.broadcast_to(seen_p[HALO + i][0:1], (8, 128)), 0.0) for i in range(CX)], axis=1
    )
    hi, mid, lo = split3(top)
    stacked = jnp.concatenate(
        [hi.astype(F32), mid.astype(F32), lo.astype(F32), jnp.zeros((8, CX * 128), F32)], axis=0
    ).astype(BF16)
    got = lax.dot_general(
        stacked, pick[:, HALO * 128 : (HALO + CX) * 128], (((1,), (1,)), ((), ())), preferred_element_type=F32
    )
    vm[0] = got[0:8] + got[8:16] + got[16:24]
    copies_z = [
        pltpu.make_async_remote_copy(
            vm.at[0], zbuf.at[dz - 1], z_s, z_r,
            device_id=place(dz=dz), device_id_type=MESH,
        )
        for dz in range(1, NZC)
    ]
    for copy in copies_z:
        copy.start()
    thin_p = thin_solve(False)
    for copy in copies_a[0]:
        copy.start()


    def coef_row(r, carry):
        s = cext[r]
        fm, fp = x_inside(r)
        hxm = harmonic(s, cext[r - 1]) * fm
        hxp = harmonic(s, cext[r + 1]) * fp
        hym = jnp.where(in_ym, harmonic(s, pltpu.roll(s, 1, 0)), 0.0)
        hyp = jnp.where(in_yp, harmonic(s, pltpu.roll(s, EY - 1, 0)), 0.0)
        hzm = jnp.where(in_zm, harmonic(s, pltpu.roll(s, 1, 1)), 0.0)
        hzp = jnp.where(in_zp, harmonic(s, pltpu.roll(s, 127, 1)), 0.0)
        diag = hxm + hxp + hym + hyp + hzm + hzp
        diag = diag + s * ((1.0 - fm) + (1.0 - fp))
        diag = diag + jnp.where(in_ym, 0.0, s) + jnp.where(in_yp, 0.0, s) + jnp.where(in_zp, 0.0, s)
        inv = 1.0 / diag
        for i, h in enumerate((hxm, hxp, hym, hyp, hzm, hzp)):
            coef[i, r] = h * inv
        return carry

    lax.fori_loop(1, EX - 1, coef_row, 0, unroll=2)

    def slope_of(s, n):
        total = s + n
        return 2.0 * n * n / (total * total)

    def slope_row(r, carry):
        s = cext[r]
        fm, fp = x_inside(r)
        q = r - HALO
        slope[0, q] = slope_of(s, cext[r - 1]) * fm + (1.0 - fm)
        slope[1, q] = slope_of(s, cext[r + 1]) * fp + (1.0 - fp)
        slope[2, q] = jnp.where(in_ym, slope_of(s, pltpu.roll(s, 1, 0)), 1.0)
        slope[3, q] = jnp.where(in_yp, slope_of(s, pltpu.roll(s, EY - 1, 0)), 1.0)
        slope[4, q] = jnp.where(in_zm, slope_of(s, pltpu.roll(s, 1, 1)), 0.0)
        slope[5, q] = jnp.where(in_zp, slope_of(s, pltpu.roll(s, 127, 1)), 1.0)
        return carry

    def app(slot, x, prev, dest, wc, wu, wp, e):
        rows = CX + 2 * e
        block = BLOCKS[rows]

        def step(q, carry):
            fresh = []
            for i in range(block):
                r = HALO - e + q * block + i
                u = x[slot, r]
                total = coef[0, r] * x[slot, r - 1] + coef[1, r] * x[slot, r + 1]
                total = total + coef[2, r] * pltpu.roll(u, 1, 0) + coef[3, r] * pltpu.roll(u, EY - 1, 0)
                total = total + coef[4, r] * pltpu.roll(u, 1, 1) + coef[5, r] * pltpu.roll(u, 127, 1)
                value = wu * u + wc * total
                if prev is not None:
                    value = value - wp * prev[slot, r]
                fresh.append((r, value))
            for r, value in fresh:
                dest[slot, r] = value
            return carry

        lax.fori_loop(0, rows // block, step, 0)

    def full_solve(which, slot, x0, x1):
        settle(x0.at[slot], warm_r.at[which, slot])
        app(slot, x0, None, x1, 1.0 / centre, 1.0 - 1.0 / centre, 0.0, HALO - 1)
        for k, (a, b) in enumerate(STEPS):
            older, newer = (x1, x0) if k % 2 else (x0, x1)
            app(slot, newer, older, older, b, 1.0 + a - b, a, HALO - 2 - k)

    pot, adj = p1, a1
    full_solve(0, 0, p0, p1)

    settle(zbuf, z_r)
    total = vm[0]
    for i in range(NZC - 1):
        total = total + zbuf[i]
    vm[1] = total
    copies_g = [
        pltpu.make_async_remote_copy(
            vm.at[1], gbuf.at[dg - 1], g_s, g_r,
            device_id=place(dg=dg), device_id_type=MESH,
        )
        for dg in range(1, NGY)
    ]
    for copy in copies_g:
        copy.start()
    for copy in copies_a[1]:
        copy.start()
    full_solve(0, 1, p0, p1)
    add_thin(thin_p, pot)

    lax.fori_loop(HALO, HALO + CX, slope_row, 0, unroll=2)
    full_solve(1, 0, a0, a1)


    full_solve(1, 1, a0, a1)
    settle(gbuf, g_r)
    total = vm[1]
    for i in range(NGY - 1):
        total = total + gbuf[i]
    sub8 = lax.broadcasted_iota(I32, (8, 128), 0)
    lane8 = lax.broadcasted_iota(I32, (8, 128), 1)
    seen = jnp.where(sub8 == 0, obs_ref[pl.ds(idents[0], 1), :], obs_ref[pl.ds(idents[1], 1), :])
    misfit = jnp.where(sub8 < 2, total - seen, 0.0)
    hi, mid, lo = split3(misfit)
    stacked = jnp.concatenate(
        [hi.astype(F32), mid.astype(F32), lo.astype(F32), jnp.zeros((8, 128), F32)], axis=0
    ).astype(BF16)
    back = jnp.dot(stacked, pick[...], preferred_element_type=F32)
    for r in range(1, EX - 1):
        cut = back[:, r * 128 : (r + 1) * 128]
        both = cut[0:8] + cut[8:16] + cut[16:24]
        line = jnp.where(lane8[0:1] < 64, both[0:1], both[1:2])
        srhs[r - 1] = jnp.where(sub8 == 0, line, 0.0)
    thin_a = thin_solve(False)
    add_thin(thin_a, adj)

    def grad_row(r, carry):
        q = r - HALO
        fm, fp = x_inside(r)
        sums = [jnp.zeros((EY, 128), F32) for _ in range(6)]
        for slot in range(2):
            p = pot[slot, r]
            a = adj[slot, r]
            near = [
                (pot[slot, r - 1] * fm, adj[slot, r - 1] * fm),
                (pot[slot, r + 1] * fp, adj[slot, r + 1] * fp),
            ]
            for inside, shift, axis in ((in_ym, 1, 0), (in_yp, EY - 1, 0), (in_zm, 1, 1), (in_zp, 127, 1)):
                near.append(
                    (
                        jnp.where(inside, pltpu.roll(p, shift, axis), 0.0),
                        jnp.where(inside, pltpu.roll(a, shift, axis), 0.0),
                    )
                )
            sums = [old + (p - pn) * (a - an) for old, (pn, an) in zip(sums, near)]
        out = slope[0, q] * sums[0]
        for i in range(1, 6):
            out = out + slope[i, q] * sums[i]
        pan8[q] = out[HALO : HALO + YR]
        return carry

    pan8 = slope.at[0, :, 0:YR, :]

    for c in range(2):
        lax.fori_loop(HALO + XR * c, HALO + XR * c + XR, grad_row, 0, unroll=2)
        gt[c] = jnp.transpose(slope[0, XR * c : XR * c + XR, 0:YR, :].reshape(128, 128))
        for ds in range(1, NSRCG):
            s2 = lax.rem(src + ds, NSRCG)
            pltpu.make_async_remote_copy(
                gt.at[c, pl.ds(pl.multiple_of(16 * s2, 16), 16), :],
                rbuf.at[lax.rem(core + c, 2), ds],
                rs_s, rs_r,
                device_id={"src": s2, "gx": 2 * zc + c, "gy": gy}, device_id_type=MESH,
            ).start()
    pltpu.make_async_remote_copy(
        gt.at[1 - core, own_rows, :], rbuf.at[1, 0], rs_s, rs_r,
        device_id=place(t=1), device_id_type=MESH,
    ).start()
    pltpu.make_async_copy(gt.at[core, own_rows, :], rbuf.at[0, 0], rs_r).start()
    settle(rbuf, rs_r)
    total = rbuf[0, 0] + rbuf[1, 0]
    for ds in range(1, NSRCG):
        total = total + (rbuf[0, ds] + rbuf[1, ds])
    total = -total
    for x in range(XR):
        out_ref[x] = (pltpu.roll(total, 128 - YR * x, 1) if x else total)[:, :YR]

    sent = p0.at[:, 0:16, 0:YR, :]
    for which in range(2):
        for slot in range(2):
            settle(sent, warm_s.at[which, slot])
    settle(sent, cond_s)
    settle(gath.at[0 : 16 * (NSRCG - 1), :], src_s)
    settle(thin_main.at[0 : 5 * XR], main_s)
    settle(thin_edge, edge_s)
    settle(zbuf, z_s)
    settle(gbuf, g_s)
    settle(gt.at[:, 0 : 8 * (2 * NSRCG - 1), :], rs_s)


def body(warm_potential, warm_adjoint, conductivity, electrodes, receivers, observed, source_order):
    xr, yr, depth = conductivity.shape
    hbm = pl.BlockSpec(memory_space=pltpu.HBM)
    vmem = pl.BlockSpec(memory_space=pltpu.VMEM)
    field = pltpu.VMEM((2, EX, EY, 128), F32)
    thin = pltpu.VMEM((EX, 8, 128), F32)
    inner = pltpu.VMEM((EX - 2, 8, 128), F32)
    dma = pltpu.SemaphoreType.DMA
    result = pl.pallas_call(
        kernel,
        out_shape=jax.ShapeDtypeStruct((xr, depth, yr), F32),
        in_specs=[hbm] * 7,
        out_specs=vmem,
        scratch_shapes=[
            pltpu.VMEM((xr, depth, yr), F32),
            pltpu.VMEM((depth, xr * yr), F32),
            pltpu.SMEM((2, 32), I32),
            pltpu.VMEM((2, 128), I32),
            pltpu.VMEM((32, 128), F32),
            pltpu.SMEM((32,), I32),
            field, field, field, field,
            pltpu.VMEM((EX, EY, 128), F32),
            pltpu.VMEM((6, EX, EY, 128), F32),
            pltpu.VMEM((6, CX, EY, 128), F32),
            pltpu.VMEM((128, 128), F32),
            pltpu.VMEM((XR, YR, 128), F32),
            pltpu.VMEM((128, EX * 128), BF16),
            pltpu.VMEM((4, XR, YR, 128), F32),
            pltpu.VMEM((XR, 8, 128), F32),
            pltpu.VMEM((2, 8, 128), F32),
            thin,
            pltpu.VMEM((2, 6, 8, 128), F32),
            thin,
            pltpu.VMEM((6, EX - 2, 8, 128), F32),
            inner, inner, thin, thin,
            pltpu.VMEM((2, 8, 128), F32),
            pltpu.VMEM((NZC - 1, 8, 128), F32),
            pltpu.VMEM((NGY - 1, 8, 128), F32),
            pltpu.VMEM((2, 128, 128), F32),
            pltpu.VMEM((2, NSRCG, 16, 128), F32),
            dma, dma, dma, dma,
            dma((6,)),
            dma((2, 2)), dma((2, 2)),
            *([dma] * 10),
        ],
        compiler_params=pltpu.CompilerParams(
            collective_id=0, has_side_effects=True, vmem_limit_bytes=63 * 1024 * 1024
        ),
    )(
        warm_potential, warm_adjoint, jnp.transpose(conductivity, (0, 2, 1)), electrodes.T, receivers.T,
        observed, source_order,
    )
    return jnp.transpose(result, (0, 2, 1))


def solution(mesh):
    in_specs = (
        P("src", "gx", "gy", None),
        P("src", "gx", "gy", None),
        P("gx", "gy", "src"),
        P(),
        P(),
        P(),
        P(),
    )
    out_specs = P("gx", "gy", "src")
    return jax.shard_map(body, mesh=mesh, in_specs=in_specs, out_specs=out_specs, check_vma=False)
```
